32 devices in a mesh: gx: 16 (over z, x, core), gy: 2 (over y).
Axes of the slice: x: 2, y: 2, z: 4, core: 2. Of those that a mesh axis runs over, the one named last changes fastest.
Arguments:
- potential: float32 [3, 1, 4096, 256], P(None, None, 'gx', 'gy'), may hold values from -8 to 8
- labels: int32 [1, 4096, 256], P(None, 'gx', 'gy'), may hold values from 0 to 7
- principal: float32 [2, 8], replicated, may hold values from 0.5 to 16
- off_diagonal: float32 [3, 8], replicated, may hold values from -0.4 to 0.4
Outputs:
- updated: float32 [3, 1, 4096, 256], P(None, None, 'gx', 'gy')
The draws below stay inside these ranges and needn't reach their ends.
All inputs are finite; a program needn't handle non-finite values.
Results may differ from the reference program's by a relative error of at most 0.0017.
Values sent between devices are 32-bit elements; how exact they have to be, the bound alone decides.
A program may use at most 64 MiB of HBM per device.

```python
import math
import jax
import jax.numpy as jnp
from jax import lax

NX = 4096
CY = 128
NZ = 1
LOADS = 3
PHASES = 8
NY = 256


def draw_potential(key, part):
    key_rough, key_shift, key_angle = jax.random.split(key, 3)
    dims_all = (LOADS, NZ, NX, NY)
    rough_part = jax.random.truncated_normal(key_rough, -3.0, 3.0, dims_all, jnp.float32)
    shifted = jax.random.uniform(key_shift, (LOADS, NZ, 1, 1), jnp.float32, -1.5, 1.5)
    phase_angle = jax.random.uniform(key_angle, (LOADS, NZ, 1, 1), jnp.float32, -math.pi, math.pi)
    position = jnp.arange(NX, dtype=jnp.float32)[None, None, :, None]
    long_wave = 3.0 * jnp.sin(position * (2.0 * math.pi / NX) + phase_angle)
    return rough_part + shifted + long_wave


def draw_principal(key, part):
    key_along, key_across = jax.random.split(key)
    along_x = jnp.exp(jax.random.uniform(key_along, (1, PHASES), jnp.float32, math.log(8.0), math.log(16.0)))
    along_y = jnp.exp(jax.random.uniform(key_across, (1, PHASES), jnp.float32, math.log(0.5), math.log(16.0)))
    return jnp.concatenate([along_x, along_y], 0)


def plant(array, stream_key, least, high):
    shape = array.shape
    place = [jax.random.randint(jax.random.fold_in(stream_key, axis), (), 0, shape[axis]) for axis in range(len(shape))]
    array = array.at[tuple(place)].set(least)
    longest = shape.index(max(shape))
    place[longest] = (place[longest] + 1) % shape[longest]
    return array.at[tuple(place)].set(high)


def setup_inputs(seed: int = 0) -> dict:
    seeds = jax.random.split(jax.random.key(seed), 5)
    potential = draw_potential(jax.random.fold_in(seeds[4], 71), 0)
    labels = plant(jax.random.randint(seeds[1], (NZ, NX, NY), 0, PHASES), jax.random.fold_in(seeds[1], 1), 0, PHASES - 1).astype(jnp.int32)
    principal = draw_principal(jax.random.fold_in(seeds[4], 71), 0)
    off_diagonal = jnp.clip(jax.random.uniform(seeds[3], (3, PHASES), jnp.float32, -0.4, 0.4), -0.4, 0.4)
    return dict(potential=potential, labels=labels, principal=principal, off_diagonal=off_diagonal)


def harmonic(first, second):
    return 2.0 * first * second / (first + second)


def cyclic_reduce(sub_diag, main_diag, super_diag, forcing, axis_dim):
    extent = sub_diag.shape[axis_dim]
    stride = 1
    while stride < extent:
        low_before = jnp.roll(sub_diag, stride, axis_dim)
        main_before = jnp.roll(main_diag, stride, axis_dim)
        high_before = jnp.roll(super_diag, stride, axis_dim)
        rest_before = jnp.roll(forcing, stride, axis_dim + 1)
        low_after = jnp.roll(sub_diag, -stride, axis_dim)
        main_after = jnp.roll(main_diag, -stride, axis_dim)
        high_after = jnp.roll(super_diag, -stride, axis_dim)
        rest_after = jnp.roll(forcing, -stride, axis_dim + 1)
        factor_low = -sub_diag / main_before
        factor_high = -super_diag / main_after
        forcing = forcing + factor_low[None] * rest_before + factor_high[None] * rest_after
        main_diag = main_diag + factor_low * high_before + factor_high * low_after
        sub_diag = factor_low * low_before
        super_diag = factor_high * high_after
        stride = stride * 2
    return forcing / (sub_diag + main_diag + super_diag)[None]


def central(values, axis_dim):
    return 0.5 * (jnp.roll(values, -1, axis_dim) - jnp.roll(values, 1, axis_dim))


def reference(potential, labels, principal, off_diagonal):
    damping = 2.0 / (CY * CY)
    components = jnp.concatenate([principal, off_diagonal], 0)

    def one_plane(pair):
        plane_field, plane_labels = pair
        tensor = components[:, plane_labels]
        face_east = harmonic(tensor[0], jnp.roll(tensor[0], -1, 0))
        face_west = jnp.roll(face_east, 1, 0)
        source_x = jnp.stack([face_east - face_west, central(tensor[2], 0), central(tensor[3], 0)])
        half_step = cyclic_reduce(-face_west, damping + face_west + face_east, -face_east,
                                  damping * plane_field + source_x, 0)
        face_north = harmonic(tensor[1], jnp.roll(tensor[1], -1, 1))
        face_south = jnp.roll(face_north, 1, 1)
        source_y = jnp.stack([central(tensor[2], 1), face_north - face_south, central(tensor[4], 1)])
        return cyclic_reduce(-face_south, damping + face_south + face_north, -face_north,
                             damping * half_step + source_y, 1)

    result = lax.map(one_plane, (jnp.moveaxis(potential, 1, 0), labels))
    return jnp.moveaxis(result, 0, 1)
```

```python
import functools

import jax
import jax.numpy as jnp
from jax import lax
from jax.experimental import pallas as pl
from jax.experimental.pallas import tpu as pltpu
from jax.sharding import PartitionSpec as P

MESH = pl.DeviceIdType.MESH
ROWS = 8


def sublane(shape):
    return lax.broadcasted_iota(jnp.int32, shape, len(shape) - 2)


def turn(x, by):
    size = x.shape[0]
    by = by % size
    return x if by == 0 else pltpu.roll(x, by, 0)


def following(q, last):
    wrap = turn(q[0], -1)
    wrap = jnp.where(sublane(wrap.shape) == 7, last, wrap)
    return wrap[None] if q.shape[0] == 1 else jnp.concatenate([q[1:], wrap[None]], 0)


def preceding(q):
    wrap = turn(q[-1], 1)
    first = jnp.where(sublane(wrap.shape) == 0, 0.0, wrap)[None]
    return (first if q.shape[0] == 1 else jnp.concatenate([first, q[:-1]], 0)), wrap


def split(q):
    pairs = q.reshape((q.shape[0] // 2, 2) + q.shape[1:])
    return pairs[:, 0], pairs[:, 1]


def merge(even, odd):
    return jnp.stack([even, odd], 1).reshape((2 * even.shape[0],) + even.shape[1:])


def wide(parts):
    return parts[0] if len(parts) == 1 else jnp.concatenate(parts, -1)


def strided(ref, steps):
    return jnp.stack([ref[pl.ds(t, 8, stride=steps), :] for t in range(steps)], 0)


def strided_wide(ref, steps):
    return wide([strided(ref.at[c], steps) for c in range(ref.shape[0])])


def put_wide(ref, value):
    for c in range(ref.shape[0]):
        ref[c] = value[:, c * 128 : (c + 1) * 128]


def lookup(tab, row, labels):
    out = jnp.broadcast_to(tab(row, 0), labels.shape)
    for phase in range(1, 8):
        out = jnp.where(labels == phase, jnp.broadcast_to(tab(row, phase), labels.shape), out)
    return out


def faces(k):
    nxt = following(k, k[0])
    e = 2.0 * k * nxt / (k + nxt)
    steps = k.shape[0]
    position = lax.broadcasted_iota(jnp.int32, k.shape, 0)
    return jnp.where((position == steps - 1) & (sublane(k.shape) == 7), 0.0, e)


def factor(e, damping):
    g = jnp.full(e.shape, damping, jnp.float32)
    levels = []
    g_end = jnp.zeros(e.shape[1:], jnp.float32)
    top = True
    while e.shape[0] > 1:
        e_even, e_odd = split(e)
        g_even, g_odd = split(g)
        r = 1.0 / (e_even + e_odd + g_odd)
        if top:
            is_end = (lax.broadcasted_iota(jnp.int32, r.shape, 0) == r.shape[0] - 1) & (sublane(r.shape) == 7)
            r = jnp.where(is_end, 0.0, r)
            right = jnp.where(is_end, 1.0, e_odd * r)
        else:
            right = e_odd * r
        left = e_even * r
        top = False
        levels.append((left, right, r))
        e = e_even * right
        moved, wrap = preceding(right * g_odd)
        g = g_even + left * g_odd + moved
        g_end = g_end + wrap
    e, g = e[0], g[0]
    sub = sublane(e.shape)
    for by in (1, 2, 4):
        chosen = sub % (2 * by) == by
        e_left = turn(e, by)
        r = jnp.where(chosen, 1.0 / (e_left + e + g), 0.0)
        left, right = e_left * r, e * r
        levels.append((left, right, r))
        e = e * turn(right, -by)
        wrap = turn(right * g, by)
        g = g + turn(left * g, -by) + jnp.where(sub == 0, 0.0, wrap)
        g_end = g_end + wrap
    return levels, e, g, g_end


def forward(levels, f):
    kept = []
    f_end = jnp.zeros(f.shape[1:], jnp.float32)
    for left, right, r in levels[:-3]:
        f_even, f_odd = split(f)
        kept.append(f_odd * r)
        moved, wrap = preceding(right * f_odd)
        f = f_even + left * f_odd + moved
        f_end = f_end + wrap
    f = f[0]
    sub = sublane(f.shape)
    for by, (left, right, r) in zip((1, 2, 4), levels[-3:]):
        kept.append(f * r)
        wrap = turn(right * f, by)
        f = f + turn(left * f, -by) + jnp.where(sub == 0, 0.0, wrap)
        f_end = f_end + wrap
    return kept, f, f_end


def backward(levels, kept, first, last):
    shape = kept[-1].shape
    sub = sublane(shape)
    v = jnp.broadcast_to(first, shape)
    last = jnp.broadcast_to(last, shape)
    for by, (left, right, r), own in zip((4, 2, 1), levels[:-4:-1], kept[:-4:-1]):
        after = jnp.where(sub >= 8 - by, last, turn(v, -by))
        v = jnp.where(sub % (2 * by) == by, own + left * turn(v, by) + right * after, v)
    v = v[None]
    for (left, right, r), own in zip(levels[:-3][::-1], kept[:-3][::-1]):
        odd = own + left * v + right * following(v, last)
        v = merge(v, odd)
    return v


def central(k):
    return 0.5 * (following(k, jnp.zeros_like(k[0])) - preceding(k)[0])


def put_record(box, me, rows):
    base = pl.multiple_of(me * len(rows), ROWS)
    rows = jnp.concatenate(rows, 0)
    for c in range(box.shape[0]):
        box[c, pl.ds(base, rows.shape[0]), :] = rows[:, c * 128 : (c + 1) * 128]


def matrix_rows(e, g, g_end, k, a):
    return [e[0:1], g[0:1], g_end[0:1], k[0, 0:1], k[-1, 7:8], a[0, 0:1], a[-1, 7:8], jnp.zeros_like(e[0:1])]


def forcing_rows(solved, b):
    return [s[1][0:1] for s in solved] + [s[2][0:1] for s in solved] + [b[0, 0:1], b[-1, 7:8]]


def copies(box, me, n, axis, send, recv):
    out = []
    rows = box.shape[1] // n
    for d in range(1, n):
        slot = box.at[:, pl.ds(pl.multiple_of(me * rows, ROWS), rows), :]
        out.append(
            pltpu.make_async_remote_copy(
                src_ref=slot,
                dst_ref=slot,
                send_sem=send.at[d],
                recv_sem=recv.at[d],
                device_id={axis: lax.rem(me + d, n)},
                device_id_type=MESH,
            )
        )
    return out


def get_row(box, n, q):
    parts = []
    rows = box.shape[1] // n
    for c in range(box.shape[0]):
        if n >= 8:
            parts.append(box[c, pl.ds(q, n, stride=rows), :])
            continue
        sub = sublane((8, 128)) % n
        out = jnp.broadcast_to(box[c, q : q + 1, :], (8, 128))
        for i in range(1, n):
            out = jnp.where(sub == i, box[c, i * rows + q : i * rows + q + 1, :], out)
        parts.append(out)
    return wide(parts)


def ring_factor(box, n):
    e, g, g_end, k_head, k_tail, a_head, a_tail = [get_row(box, n, q) for q in range(7)]
    k_next = turn(k_head, -1)
    link = 2.0 * k_tail * k_next / (k_tail + k_next)
    gain = [link, 0.5 * turn(a_head, -1)]
    loss = [turn(link, 1), turn(0.5 * a_tail, 1)]
    r = 1.0 / (e + link + g_end)
    left, right = e * r, link * r
    g = g + left * g_end + turn(right * g_end, 1)
    e = e * right
    levels = []
    by = 1
    while by < n:
        e_left = turn(e, by)
        s = 1.0 / (e_left + e + g)
        lo, hi = e_left * s, e * s
        levels.append((by, lo, hi))
        g = g + turn(lo * g, -by) + turn(hi * g, by)
        e = e * turn(hi, -by)
        by *= 2
    return gain, loss, r, left, right, levels, 1.0 / g


def ring_solve(box, n, skip, ring, order, me, first_out, last_out):
    gain, loss, r, left, right, levels, inv = ring
    f = [get_row(box, n, skip + q) for q in range(3)]
    f_end = [get_row(box, n, skip + q) for q in range(3, 6)]
    b_head, b_tail = get_row(box, n, skip + 6), get_row(box, n, skip + 7)
    gain = gain + [0.5 * turn(b_head, -1)]
    loss = loss + [turn(0.5 * b_tail, 1)]
    size = inv.shape[0]
    for i, which in enumerate(order):
        end = f_end[i] + gain[which]
        v = f[i] - loss[which] + left * end + turn(right * end, 1)
        for by, lo, hi in levels:
            v = v + turn(lo * v, -by) + turn(hi * v, by)
        v = v * inv
        first_out[i * size : (i + 1) * size, :] = v
        last_out[i * size : (i + 1) * size, :] = r * end + left * v + right * turn(v, -1)
    return [
        (first_out[pl.ds(i * size + me, 1), :], last_out[pl.ds(i * size + me, 1), :]) for i in range(3)
    ]


def kernel(nx, ny, damping, pot_hbm, lab_hbm, pri_hbm, off_hbm, out, pot, lab, pri, off, box_x, mat_y, box_y, labt, ft,
           first_x, last_x, first_y, last_y, send_x, recv_x, send_y, recv_y,
           send_my, recv_my, load):
    me_x, me_y = lax.axis_index("gx"), lax.axis_index("gy")
    barrier = pltpu.get_barrier_semaphore()
    for d in range(1, nx):
        pl.semaphore_signal(barrier, inc=1, device_id={"gx": lax.rem(me_x + d, nx)}, device_id_type=MESH)
    for d in range(1, ny):
        pl.semaphore_signal(barrier, inc=1, device_id={"gy": lax.rem(me_y + d, ny)}, device_id_type=MESH)

    loads = [
        pltpu.make_async_copy(src, dst, load.at[i])
        for i, (src, dst) in enumerate(((lab_hbm, lab), (pri_hbm, pri), (off_hbm, off), (pot_hbm, pot)))
    ]
    for copy in loads:
        copy.start()
    def tab(row, phase):
        ref, row = (pri, row) if row < 2 else (off, row - 2)
        return ref[row : row + 1, phase : phase + 1]

    rows, cols = lab.shape
    steps = rows // 8
    for copy in loads[:3]:
        copy.wait()
    labels = strided(lab, steps)
    k, a = lookup(tab, 0, labels), lookup(tab, 2, labels)
    e = faces(k)
    levels, e_in, g, g_end = factor(e, damping)
    b = lookup(tab, 3, labels)
    source = [e - preceding(e)[0], central(a), central(b)]
    loads[3].wait()
    solved = [forward(levels, damping * strided(pot.at[i], steps) + source[i]) for i in range(3)]
    put_record(box_x, me_x, matrix_rows(e_in, g, g_end, k, a) + forcing_rows(solved, b))
    pl.semaphore_wait(barrier, nx - 1 + ny - 1)
    sent_x = copies(box_x, me_x, nx, "gx", send_x, recv_x)
    for copy in sent_x:
        copy.start()

    lanes = labt.shape[0] * 128
    repeat = lanes // rows

    def across(q):
        flat = q.reshape(rows, cols)
        if repeat > 1:
            flat = jnp.concatenate([flat] * repeat, 0)
        return flat.T

    put_wide(labt, across(labels))
    ysteps = cols // 8
    labels_y = strided_wide(labt, ysteps)
    ky, ay, by = lookup(tab, 1, labels_y), lookup(tab, 2, labels_y), lookup(tab, 4, labels_y)
    ey = faces(ky)
    levels_y, ey_in, gy, gy_end = factor(ey, damping)
    put_record(mat_y, me_y, matrix_rows(ey_in, gy, gy_end, ky, ay))
    sent_my = copies(mat_y, me_y, ny, "gy", send_my, recv_my)
    for copy in sent_my:
        copy.start()
    source_y = [central(ay), ey - preceding(ey)[0], central(by)]

    for copy in sent_x:
        copy.wait_recv()
    ring_x = ring_factor(box_x, nx)
    ends = ring_solve(box_x, nx, ROWS, ring_x, (0, 1, 2), me_x, first_x, last_x)
    solved_y = []
    for i in range(3):
        half = backward(levels, solved[i][0], *ends[i])
        put_wide(ft.at[i], across(half))
        solved_y.append(forward(levels_y, damping * strided_wide(ft.at[i], ysteps) + source_y[i]))
    put_record(box_y, me_y, forcing_rows(solved_y, by))
    sent_y = copies(box_y, me_y, ny, "gy", send_y, recv_y)
    for copy in sent_y:
        copy.start()
    for copy in sent_my:
        copy.wait_recv()
    ring_y = ring_factor(mat_y, ny)
    for copy in sent_y:
        copy.wait_recv()
    ends = ring_solve(box_y, ny, 0, ring_y, (1, 0, 2), me_y, first_y, last_y)
    for i in range(3):
        v = backward(levels_y, solved_y[i][0], *ends[i])
        for t in range(ysteps):
            for c in range(lanes // 128):
                ft[i, c, pl.ds(t, 8, stride=ysteps), :] = v[t, :, c * 128 : (c + 1) * 128]
        back = jnp.concatenate([ft[i, c].T for c in range(lanes // 128)], 0)[:rows].reshape(steps, 8, cols)
        for t in range(steps):
            out[i, pl.ds(t, 8, stride=steps), :] = back[t]
    for copy in sent_x + sent_my + sent_y:
        copy.wait_send()


def local(potential, labels, principal, off_diagonal):
    nx, ny = lax.axis_size("gx"), lax.axis_size("gy")
    loads, _, rows, cols = potential.shape
    lanes = max(rows, 128)
    damping = 2.0 / (cols * cols)
    vmem = pl.BlockSpec(memory_space=pltpu.VMEM)
    hbm = pl.BlockSpec(memory_space=pltpu.HBM)
    result = pl.pallas_call(
        functools.partial(kernel, nx, ny, damping),
        out_shape=pltpu.VMEM((loads, rows, cols), jnp.float32),
        in_specs=[hbm] * 4,
        out_specs=vmem,
        scratch_shapes=[
            pltpu.VMEM((loads, rows, cols), jnp.float32),
            pltpu.VMEM((rows, cols), jnp.int32),
            pltpu.VMEM(principal.shape, jnp.float32),
            pltpu.VMEM(off_diagonal.shape, jnp.float32),
            pltpu.VMEM((1, nx * 2 * ROWS, cols), jnp.float32),
            pltpu.VMEM((lanes // 128, ny * ROWS, 128), jnp.float32),
            pltpu.VMEM((lanes // 128, ny * ROWS, 128), jnp.float32),
            pltpu.VMEM((lanes // 128, cols, 128), jnp.int32),
            pltpu.VMEM((loads, lanes // 128, cols, 128), jnp.float32),
            pltpu.VMEM((loads * max(nx, 8), cols), jnp.float32),
            pltpu.VMEM((loads * max(nx, 8), cols), jnp.float32),
            pltpu.VMEM((loads * max(ny, 8), lanes), jnp.float32),
            pltpu.VMEM((loads * max(ny, 8), lanes), jnp.float32),
            pltpu.SemaphoreType.DMA((nx,)),
            pltpu.SemaphoreType.DMA((nx,)),
            pltpu.SemaphoreType.DMA((ny,)),
            pltpu.SemaphoreType.DMA((ny,)),
            pltpu.SemaphoreType.DMA((ny,)),
            pltpu.SemaphoreType.DMA((ny,)),
            pltpu.SemaphoreType.DMA((4,)),
        ],
        compiler_params=pltpu.CompilerParams(
            collective_id=0, has_side_effects=True, vmem_limit_bytes=32 * 1024 * 1024
        ),
    )(*[pltpu.with_memory_space_constraint(x, pltpu.HBM) for x in (potential.reshape(loads, rows, cols), labels.reshape(rows, cols), principal, off_diagonal)])
    return result.reshape(potential.shape)


def solution(mesh):
    in_specs = (P(None, None, "gx", "gy"), P(None, "gx", "gy"), P(), P())
    out_specs = P(None, None, "gx", "gy")
    return jax.shard_map(local, mesh=mesh, in_specs=in_specs, out_specs=out_specs, check_vma=False)
```

```python
import functools

import jax
import jax.numpy as jnp
from jax import lax
from jax.experimental import pallas as pl
from jax.experimental.pallas import tpu as pltpu
from jax.sharding import PartitionSpec as P

MESH = pl.DeviceIdType.MESH
ROWS = 8


def sublane(shape):
    return lax.broadcasted_iota(jnp.int32, shape, len(shape) - 2)


def turn(x, by):
    size = x.shape[0]
    by = by % size
    return x if by == 0 else pltpu.roll(x, by, 0)


def following(q, last):
    wrap = turn(q[0], -1)
    wrap = jnp.where(sublane(wrap.shape) == 7, last, wrap)
    return wrap[None] if q.shape[0] == 1 else jnp.concatenate([q[1:], wrap[None]], 0)


def preceding(q):
    wrap = turn(q[-1], 1)
    first = jnp.where(sublane(wrap.shape) == 0, 0.0, wrap)[None]
    return (first if q.shape[0] == 1 else jnp.concatenate([first, q[:-1]], 0)), wrap


def split(q):
    pairs = q.reshape((q.shape[0] // 2, 2) + q.shape[1:])
    return pairs[:, 0], pairs[:, 1]


def merge(even, odd):
    return jnp.stack([even, odd], 1).reshape((2 * even.shape[0],) + even.shape[1:])


def wide(parts):
    return parts[0] if len(parts) == 1 else jnp.concatenate(parts, -1)


def strided(ref, steps):
    return jnp.stack([ref[pl.ds(t, 8, stride=steps), :] for t in range(steps)], 0)


def strided_wide(ref, steps):
    return wide([strided(ref.at[c], steps) for c in range(ref.shape[0])])


def put_wide(ref, value):
    for c in range(ref.shape[0]):
        ref[c] = value[:, c * 128 : (c + 1) * 128]


def get_wide(ref):
    return wide([ref[c] for c in range(ref.shape[0])])


def spread(ref, row):
    lane = lax.broadcasted_iota(jnp.int32, (8, 128), 1)
    out = jnp.broadcast_to(ref[row : row + 1, 0:1], (8, 128))
    for phase in range(1, 8):
        out = jnp.where(lane == phase, jnp.broadcast_to(ref[row : row + 1, phase : phase + 1], (8, 128)), out)
    return out


def lookup(table, labels):
    width = labels.shape[-1]
    flat = labels.reshape(-1, 8, width)
    out = []
    for t in range(flat.shape[0]):
        parts = [
            jnp.take_along_axis(table, flat[t, :, c : c + 128], axis=1, mode="promise_in_bounds")
            for c in range(0, width, 128)
        ]
        out.append(wide(parts))
    return jnp.stack(out, 0).reshape(labels.shape)


def faces(half_inverse):
    e = 1.0 / (half_inverse + following(half_inverse, half_inverse[0]))
    position = lax.broadcasted_iota(jnp.int32, e.shape, 0)
    return jnp.where((position == e.shape[0] - 1) & (sublane(e.shape) == 7), 0.0, e)


def factor(e, damping):
    g = jnp.full(e.shape, damping, jnp.float32)
    levels = []
    g_end = jnp.zeros(e.shape[1:], jnp.float32)
    top = True
    while e.shape[0] > 1:
        e_even, e_odd = split(e)
        g_even, g_odd = split(g)
        r = 1.0 / (e_even + e_odd + g_odd)
        if top:
            is_end = (lax.broadcasted_iota(jnp.int32, r.shape, 0) == r.shape[0] - 1) & (sublane(r.shape) == 7)
            r = jnp.where(is_end, 0.0, r)
            right = jnp.where(is_end, 1.0, e_odd * r)
        else:
            right = e_odd * r
        left = e_even * r
        top = False
        levels.append((left, right, r))
        e = e_even * right
        moved, wrap = preceding(right * g_odd)
        g = g_even + left * g_odd + moved
        g_end = g_end + wrap
    e, g = e[0], g[0]
    sub = sublane(e.shape)
    for by in (1, 2, 4):
        chosen = sub % (2 * by) == by
        e_left = turn(e, by)
        r = jnp.where(chosen, 1.0 / (e_left + e + g), 0.0)
        left, right = e_left * r, e * r
        levels.append((left, right, r))
        e = e * turn(right, -by)
        wrap = turn(right * g, by)
        g = g + turn(left * g, -by) + jnp.where(sub == 0, 0.0, wrap)
        g_end = g_end + wrap
    return levels, e, g, g_end


def forward(levels, f):
    kept = []
    f_end = jnp.zeros(f.shape[1:], jnp.float32)
    for left, right, r in levels[:-3]:
        f_even, f_odd = split(f)
        kept.append(f_odd * r)
        moved, wrap = preceding(right * f_odd)
        f = f_even + left * f_odd + moved
        f_end = f_end + wrap
    f = f[0]
    sub = sublane(f.shape)
    for by, (left, right, r) in zip((1, 2, 4), levels[-3:]):
        kept.append(f * r)
        wrap = turn(right * f, by)
        f = f + turn(left * f, -by) + jnp.where(sub == 0, 0.0, wrap)
        f_end = f_end + wrap
    return kept, f, f_end


def backward(levels, kept, first, last):
    shape = kept[-1].shape
    sub = sublane(shape)
    v = jnp.broadcast_to(first, shape)
    last = jnp.broadcast_to(last, shape)
    for by, (left, right, r), own in zip((4, 2, 1), levels[:-4:-1], kept[:-4:-1]):
        after = jnp.where(sub >= 8 - by, last, turn(v, -by))
        v = jnp.where(sub % (2 * by) == by, own + left * turn(v, by) + right * after, v)
    v = v[None]
    for (left, right, r), own in zip(levels[:-3][::-1], kept[:-3][::-1]):
        odd = own + left * v + right * following(v, last)
        v = merge(v, odd)
    return v


def homogeneous(levels):
    none = [jnp.zeros_like(r) for _, _, r in levels]
    row = jnp.zeros_like(levels[-1][2][0:1])
    return backward(levels, none, row + 1.0, row), backward(levels, none, row, row + 1.0)


def central(k):
    return 0.5 * (following(k, jnp.zeros_like(k[0])) - preceding(k)[0])


def put_record(box, me, rows):
    for q, row in enumerate(rows):
        box[q, pl.ds(me, 1), :] = row


def partner(me, mask, n):
    if n & (n - 1):
        return lax.rem(me + mask, n)
    out = me
    bit = 1
    while bit < n:
        if mask & bit:
            out = out + bit * (1 - 2 * lax.rem(lax.div(me, bit), 2))
        bit *= 2
    return out


def send_all(box, me, n, axis, send, recv):
    slot = box.at[:, pl.ds(me, 1), :]
    for mask in range(n - 1, 0, -1):
        pltpu.make_async_remote_copy(
            src_ref=slot,
            dst_ref=slot,
            send_sem=send,
            recv_sem=recv,
            device_id={axis: partner(me, mask, n)},
            device_id_type=MESH,
        ).start()


def wait_all(box, n, sem):
    rest = box.at[:, pl.ds(0, n - 1), :]
    pltpu.make_async_copy(rest, rest, sem).wait()


def get_row(box, n, q):
    if n >= 8:
        return box[q]
    width = box.shape[-1]
    sub = sublane((8, width)) % n
    out = jnp.broadcast_to(box[q, 0:1, :], (8, width))
    for i in range(1, n):
        out = jnp.where(sub == i, jnp.broadcast_to(box[q, i : i + 1, :], (8, width)), out)
    return out


def ring_factor(box, n, tables):
    e, g, g_end, head, tail = [get_row(box, n, q) for q in range(5)]
    head, tail = head.astype(jnp.int32), tail.astype(jnp.int32)
    k_table, a_table, b_table = tables
    link = 1.0 / (lookup(k_table, tail) + turn(lookup(k_table, head), -1))
    gain = [link, 0.5 * turn(lookup(a_table, head), -1), 0.5 * turn(lookup(b_table, head), -1)]
    loss = [turn(link, 1), turn(0.5 * lookup(a_table, tail), 1), turn(0.5 * lookup(b_table, tail), 1)]
    r = 1.0 / (e + link + g_end)
    left, right = e * r, link * r
    g = g + left * g_end + turn(right * g_end, 1)
    e = e * right
    levels = []
    by = 1
    while by < n:
        e_left = turn(e, by)
        s = 1.0 / (e_left + e + g)
        lo, hi = e_left * s, e * s
        levels.append((by, lo, hi))
        g = g + turn(lo * g, -by) + turn(hi * g, by)
        e = e * turn(hi, -by)
        by *= 2
    return gain, loss, r, left, right, levels, 1.0 / g


def ring_solve(box, n, ring, order, me, first_out, last_out):
    gain, loss, r, left, right, levels, inv = ring
    size = inv.shape[0]
    for i, which in enumerate(order):
        end = get_row(box, n, 3 + i) + gain[which]
        v = get_row(box, n, i) - loss[which] + left * end + turn(right * end, 1)
        for by, lo, hi in levels:
            v = v + turn(lo * v, -by) + turn(hi * v, by)
        v = v * inv
        first_out[i * size : (i + 1) * size, :] = v
        last_out[i * size : (i + 1) * size, :] = r * end + left * v + right * turn(v, -1)
    return [
        (first_out[pl.ds(i * size + me, 1), :], last_out[pl.ds(i * size + me, 1), :]) for i in range(3)
    ]


def total(x):
    x = jnp.sum(x, axis=0) if x.ndim == 3 else x
    for by in (1, 2, 4):
        x = x + turn(x, by)
    return x[0:1]


def kernel(nx, ny, damping, pot_hbm, lab_hbm, pri_hbm, off_hbm, out, pot, lab, pri, off, mat_x, box_x, mat_y, box_y,
           labt, ft, ends_y, first_x, last_x, first_y, last_y, send_x, recv_x, send_y, recv_y, load):
    me_x, me_y = lax.axis_index("gx"), lax.axis_index("gy")
    loads, steps, _, cols = pot.shape
    rows = steps * 8
    for s in range(8):
        pltpu.make_async_copy(lab_hbm.at[pl.ds(s * steps, steps), :], lab.at[:, s, :], load.at[0]).start()
    small = [pltpu.make_async_copy(src, dst, load.at[i]) for i, (src, dst) in enumerate(((pri_hbm, pri), (off_hbm, off)), 1)]
    for copy in small:
        copy.start()
    barrier = pltpu.get_barrier_semaphore()
    for mask in range(1, nx):
        pl.semaphore_signal(barrier, inc=1, device_id={"gx": partner(me_x, mask, nx)}, device_id_type=MESH)
    for mask in range(1, ny):
        pl.semaphore_signal(barrier, inc=1, device_id={"gy": partner(me_y, mask, ny)}, device_id_type=MESH)
    for s in range(8):
        pltpu.make_async_copy(pot_hbm.at[:, pl.ds(s * steps, steps), :], pot.at[:, :, s, :], load.at[3]).start()

    for copy in small:
        copy.wait()
    kx_table, ky_table = 0.5 / spread(pri, 0), 0.5 / spread(pri, 1)
    xy_table, xz_table, yz_table = [spread(off, row) for row in range(3)]
    pltpu.make_async_copy(lab, lab, load.at[0]).wait()
    labels = lab[...]
    e = faces(lookup(kx_table, labels))
    levels, e_in, g, g_end = factor(e, damping)
    head, tail = labels[0, 0:1].astype(jnp.float32), labels[-1, 7:8].astype(jnp.float32)
    put_record(mat_x, me_x, [e_in[0:1], g[0:1], g_end[0:1], head, tail])
    pl.semaphore_wait(barrier, nx - 1 + ny - 1)
    send_all(mat_x, me_x, nx, "gx", send_x.at[0], recv_x.at[0])
    a, b = lookup(xy_table, labels), lookup(xz_table, labels)
    source = [e - preceding(e)[0], central(a), central(b)]
    pltpu.make_async_copy(pot, pot, load.at[3]).wait()
    solved = [forward(levels, damping * pot[i] + source[i]) for i in range(3)]
    put_record(box_x, me_x, [s[1][0:1] for s in solved] + [s[2][0:1] for s in solved])
    send_all(box_x, me_x, nx, "gx", send_x.at[1], recv_x.at[1])

    lanes = labt.shape[0] * 128
    repeat = lanes // rows

    def across(q):
        flat = q.reshape(rows, cols)
        if repeat > 1:
            flat = jnp.concatenate([flat] * repeat, 0)
        return flat.T

    def along(q, slot):
        for t in range(ysteps):
            for c in range(lanes // 128):
                ft[slot, c, pl.ds(t, 8, stride=ysteps), :] = q[t, :, c * 128 : (c + 1) * 128]
        natural = get_wide(ft.at[slot])
        return natural, natural.T[:rows].reshape(steps, 8, cols)

    put_wide(labt, across(labels))
    ysteps = cols // 8
    labels_y = strided_wide(labt, ysteps)
    ey = faces(lookup(ky_table, labels_y))
    levels_y, ey_in, gy, gy_end = factor(ey, damping)
    head_y, tail_y = labels_y[0, 0:1].astype(jnp.float32), labels_y[-1, 7:8].astype(jnp.float32)
    put_record(mat_y, me_y, [ey_in[0:1], gy[0:1], gy_end[0:1], head_y, tail_y])
    send_all(mat_y, me_y, ny, "gy", send_y.at[0], recv_y.at[0])
    ay, by = lookup(xy_table, labels_y), lookup(yz_table, labels_y)
    source_y = [central(ay), ey - preceding(ey)[0], central(by)]
    base_y = [forward(levels_y, q) for q in source_y]
    zero = jnp.zeros((1, cols), jnp.float32)
    inner = [backward(levels, kept, zero, zero) for kept, _, _ in solved]
    first_part, last_part = homogeneous(levels)
    first_y_part, last_y_part = homogeneous(levels_y)
    first_weight, first_share = along(first_y_part, 0)
    last_weight, last_share = along(last_y_part, 1)
    first_weight, last_weight = damping * first_weight, damping * last_weight

    wait_all(mat_y, ny, recv_y.at[0])
    ring_y = ring_factor(mat_y, ny, (ky_table, xy_table, yz_table))
    wait_all(mat_x, nx, recv_x.at[0])
    ring_x = ring_factor(mat_x, nx, (kx_table, xy_table, xz_table))
    wait_all(box_x, nx, recv_x.at[1])
    ends = ring_solve(box_x, nx, ring_x, (0, 1, 2), me_x, first_x, last_x)
    turned = [across(inner[i] + first_part * ends[i][0] + last_part * ends[i][1]) for i in range(3)]
    firsts = [base_y[i][1][0:1] + total((first_weight * turned[i]).reshape(ysteps, 8, lanes)) for i in range(3)]
    lasts = [base_y[i][2][0:1] + total((last_weight * turned[i]).reshape(ysteps, 8, lanes)) for i in range(3)]
    put_record(box_y, me_y, firsts + lasts)
    send_all(box_y, me_y, ny, "gy", send_y.at[1], recv_y.at[1])

    row = jnp.zeros((1, lanes), jnp.float32)
    own = []
    for i in range(3):
        put_wide(ft.at[2 + i], turned[i])
        kept = forward(levels_y, damping * strided_wide(ft.at[2 + i], ysteps) + source_y[i])[0]
        own.append(along(backward(levels_y, kept, row, row), 2 + i)[1])
    wait_all(box_y, ny, recv_y.at[1])
    ends = ring_solve(box_y, ny, ring_y, (1, 0, 2), me_y, first_y, last_y)
    for i in range(3):
        ends_y[2 * i : 2 * i + 1, :] = ends[i][0]
        ends_y[2 * i + 1 : 2 * i + 2, :] = ends[i][1]
    column = jnp.concatenate([ends_y[...]] * 16, 0).T[:rows].reshape(steps, 8, 128)
    for i in range(3):
        for t in range(steps):
            out[i, t] = (own[i][t] + first_share[t] * column[t, :, 2 * i : 2 * i + 1]
                         + last_share[t] * column[t, :, 2 * i + 1 : 2 * i + 2])
    for box, n, sem in ((mat_x, nx, send_x.at[0]), (box_x, nx, send_x.at[1]), (mat_y, ny, send_y.at[0]), (box_y, ny, send_y.at[1])):
        wait_all(box, n, sem)


def store(v, out, sem):
    steps = v.shape[1]
    for s in range(8):
        pltpu.make_async_copy(v.at[:, :, s, :], out.at[:, pl.ds(s * steps, steps), :], sem).start()
    pltpu.make_async_copy(v, v, sem).wait()


def local(potential, labels, principal, off_diagonal):
    nx, ny = lax.axis_size("gx"), lax.axis_size("gy")
    loads, _, rows, cols = potential.shape
    lanes = max(rows, 128)
    steps = rows // 8
    damping = 2.0 / (cols * cols)
    vmem = pl.BlockSpec(memory_space=pltpu.VMEM)
    hbm = pl.BlockSpec(memory_space=pltpu.HBM)
    args = (potential.reshape(loads, rows, cols), labels.reshape(rows, cols), principal, off_diagonal)
    result = pl.pallas_call(
        functools.partial(kernel, nx, ny, damping),
        out_shape=pltpu.VMEM((loads, steps, 8, cols), jnp.float32),
        in_specs=[hbm] * 4,
        out_specs=vmem,
        scratch_shapes=[
            pltpu.VMEM((loads, steps, 8, cols), jnp.float32),
            pltpu.VMEM((steps, 8, cols), jnp.int32),
            pltpu.VMEM(principal.shape, jnp.float32),
            pltpu.VMEM(off_diagonal.shape, jnp.float32),
            pltpu.VMEM((5, nx, cols), jnp.float32),
            pltpu.VMEM((6, nx, cols), jnp.float32),
            pltpu.VMEM((5, ny, lanes), jnp.float32),
            pltpu.VMEM((6, ny, lanes), jnp.float32),
            pltpu.VMEM((lanes // 128, cols, 128), jnp.int32),
            pltpu.VMEM((5, lanes // 128, cols, 128), jnp.float32),
            pltpu.VMEM((8, lanes), jnp.float32),
            pltpu.VMEM((loads * max(nx, 8), cols), jnp.float32),
            pltpu.VMEM((loads * max(nx, 8), cols), jnp.float32),
            pltpu.VMEM((loads * max(ny, 8), lanes), jnp.float32),
            pltpu.VMEM((loads * max(ny, 8), lanes), jnp.float32),
            pltpu.SemaphoreType.DMA((2,)),
            pltpu.SemaphoreType.DMA((2,)),
            pltpu.SemaphoreType.DMA((2,)),
            pltpu.SemaphoreType.DMA((2,)),
            pltpu.SemaphoreType.DMA((4,)),
        ],
        compiler_params=pltpu.CompilerParams(
            collective_id=0, has_side_effects=True, vmem_limit_bytes=32 * 1024 * 1024
        ),
    )(*[pltpu.with_memory_space_constraint(x, pltpu.HBM) for x in args])
    result = pl.pallas_call(
        store,
        out_shape=pltpu.HBM((loads, rows, cols), jnp.float32),
        in_specs=[vmem],
        out_specs=hbm,
        scratch_shapes=[pltpu.SemaphoreType.DMA],
        compiler_params=pltpu.CompilerParams(vmem_limit_bytes=8 * 1024 * 1024),
    )(pltpu.with_memory_space_constraint(result, pltpu.VMEM))
    return result.reshape(potential.shape)


def solution(mesh):
    in_specs = (P(None, None, "gx", "gy"), P(None, "gx", "gy"), P(), P())
    out_specs = P(None, None, "gx", "gy")
    return jax.shard_map(local, mesh=mesh, in_specs=in_specs, out_specs=out_specs, check_vma=False)
```

```python
import functools

import jax
import jax.numpy as jnp
from jax import lax
from jax.experimental import pallas as pl
from jax.experimental.pallas import tpu as pltpu
from jax.sharding import PartitionSpec as P

MESH = pl.DeviceIdType.MESH
ROWS = 8


def sublane(shape):
    return lax.broadcasted_iota(jnp.int32, shape, len(shape) - 2)


def turn(x, by):
    size = x.shape[0]
    by = by % size
    return x if by == 0 else pltpu.roll(x, by, 0)


def following(q, last):
    wrap = turn(q[0], -1)
    wrap = jnp.where(sublane(wrap.shape) == 7, last, wrap)
    return wrap[None] if q.shape[0] == 1 else jnp.concatenate([q[1:], wrap[None]], 0)


def preceding(q):
    wrap = turn(q[-1], 1)
    first = jnp.where(sublane(wrap.shape) == 0, 0.0, wrap)[None]
    return (first if q.shape[0] == 1 else jnp.concatenate([first, q[:-1]], 0)), wrap


def split(q):
    pairs = q.reshape((q.shape[0] // 2, 2) + q.shape[1:])
    return pairs[:, 0], pairs[:, 1]


def merge(even, odd):
    return jnp.stack([even, odd], 1).reshape((2 * even.shape[0],) + even.shape[1:])


def wide(parts):
    return parts[0] if len(parts) == 1 else jnp.concatenate(parts, -1)


def strided(ref, steps):
    return jnp.stack([ref[pl.ds(t, 8, stride=steps), :] for t in range(steps)], 0)


def strided_wide(ref, steps):
    return wide([strided(ref.at[c], steps) for c in range(ref.shape[0])])


def put_wide(ref, value):
    for c in range(ref.shape[0]):
        ref[c] = value[:, c * 128 : (c + 1) * 128]


def get_wide(ref):
    return wide([ref[c] for c in range(ref.shape[0])])


def spread(ref, row):
    lane = lax.broadcasted_iota(jnp.int32, (8, 128), 1)
    out = jnp.broadcast_to(ref[row : row + 1, 0:1], (8, 128))
    for phase in range(1, 8):
        out = jnp.where(lane == phase, jnp.broadcast_to(ref[row : row + 1, phase : phase + 1], (8, 128)), out)
    return out


def lookup(table, labels):
    width = labels.shape[-1]
    flat = labels.reshape(-1, 8, width)
    out = []
    for t in range(flat.shape[0]):
        parts = [
            jnp.take_along_axis(table, flat[t, :, c : c + 128], axis=1, mode="promise_in_bounds")
            for c in range(0, width, 128)
        ]
        out.append(wide(parts))
    return jnp.stack(out, 0).reshape(labels.shape)


def faces(half_inverse):
    e = 1.0 / (half_inverse + following(half_inverse, half_inverse[0]))
    position = lax.broadcasted_iota(jnp.int32, e.shape, 0)
    return jnp.where((position == e.shape[0] - 1) & (sublane(e.shape) == 7), 0.0, e)


def factor(e, damping):
    g = jnp.full(e.shape, damping, jnp.float32)
    levels = []
    g_end = jnp.zeros(e.shape[1:], jnp.float32)
    top = True
    while e.shape[0] > 1:
        e_even, e_odd = split(e)
        g_even, g_odd = split(g)
        r = 1.0 / (e_even + e_odd + g_odd)
        if top:
            is_end = (lax.broadcasted_iota(jnp.int32, r.shape, 0) == r.shape[0] - 1) & (sublane(r.shape) == 7)
            r = jnp.where(is_end, 0.0, r)
            right = jnp.where(is_end, 1.0, e_odd * r)
        else:
            right = e_odd * r
        left = e_even * r
        top = False
        levels.append((left, right, r))
        e = e_even * right
        moved, wrap = preceding(right * g_odd)
        g = g_even + left * g_odd + moved
        g_end = g_end + wrap
    e, g = e[0], g[0]
    sub = sublane(e.shape)
    for by in (1, 2, 4):
        chosen = sub % (2 * by) == by
        e_left = turn(e, by)
        r = jnp.where(chosen, 1.0 / (e_left + e + g), 0.0)
        left, right = e_left * r, e * r
        levels.append((left, right, r))
        e = e * turn(right, -by)
        wrap = turn(right * g, by)
        g = g + turn(left * g, -by) + jnp.where(sub == 0, 0.0, wrap)
        g_end = g_end + wrap
    return levels, e, g, g_end


def forward(levels, f):
    kept = []
    f_end = jnp.zeros(f.shape[1:], jnp.float32)
    for left, right, r in levels[:-3]:
        f_even, f_odd = split(f)
        kept.append(f_odd * r)
        moved, wrap = preceding(right * f_odd)
        f = f_even + left * f_odd + moved
        f_end = f_end + wrap
    f = f[0]
    sub = sublane(f.shape)
    for by, (left, right, r) in zip((1, 2, 4), levels[-3:]):
        kept.append(f * r)
        wrap = turn(right * f, by)
        f = f + turn(left * f, -by) + jnp.where(sub == 0, 0.0, wrap)
        f_end = f_end + wrap
    return kept, f, f_end


def backward(levels, kept, first, last):
    shape = kept[-1].shape
    sub = sublane(shape)
    v = jnp.broadcast_to(first, shape)
    last = jnp.broadcast_to(last, shape)
    for by, (left, right, r), own in zip((4, 2, 1), levels[:-4:-1], kept[:-4:-1]):
        after = jnp.where(sub >= 8 - by, last, turn(v, -by))
        v = jnp.where(sub % (2 * by) == by, own + left * turn(v, by) + right * after, v)
    v = v[None]
    for (left, right, r), own in zip(levels[:-3][::-1], kept[:-3][::-1]):
        odd = own + left * v + right * following(v, last)
        v = merge(v, odd)
    return v


def homogeneous(levels):
    none = [jnp.zeros_like(r) for _, _, r in levels]
    row = jnp.zeros_like(levels[-1][2][0:1])
    return backward(levels, none, row + 1.0, row), backward(levels, none, row, row + 1.0)


def central(k):
    return 0.5 * (following(k, jnp.zeros_like(k[0])) - preceding(k)[0])


def matrix_rows(e, g, g_end, k, a, b):
    return [e[0:1], g[0:1], g_end[0:1]] + [q for x in (k, a, b) for q in (x[0, 0:1], x[-1, 7:8])]


def put_record(box, me, rows):
    for q, row in enumerate(rows):
        box[q, pl.ds(me, 1), :] = row


def partner(me, mask, n):
    if n & (n - 1):
        return lax.rem(me + mask, n)
    out = me
    bit = 1
    while bit < n:
        if mask & bit:
            out = out + bit * (1 - 2 * lax.rem(lax.div(me, bit), 2))
        bit *= 2
    return out


def send_all(box, me, n, axis, send, recv):
    slot = box.at[:, pl.ds(me, 1), :]
    for k in range(n - 1):
        pltpu.make_async_remote_copy(
            src_ref=slot,
            dst_ref=slot,
            send_sem=send,
            recv_sem=recv,
            device_id={axis: k + lax.div(k - me + n, n)},
            device_id_type=MESH,
        ).start()


def wait_all(box, n, sem):
    rest = box.at[:, pl.ds(0, n - 1), :]
    pltpu.make_async_copy(rest, rest, sem).wait()


def get_row(box, n, q):
    if n >= 8:
        return box[q]
    width = box.shape[-1]
    sub = sublane((8, width)) % n
    out = jnp.broadcast_to(box[q, 0:1, :], (8, width))
    for i in range(1, n):
        out = jnp.where(sub == i, jnp.broadcast_to(box[q, i : i + 1, :], (8, width)), out)
    return out


def ring_factor(box, n):
    e, g, g_end, k_head, k_tail, a_head, a_tail, b_head, b_tail = [get_row(box, n, q) for q in range(9)]
    link = 1.0 / (k_tail + turn(k_head, -1))
    gain = [link, 0.5 * turn(a_head, -1), 0.5 * turn(b_head, -1)]
    loss = [turn(link, 1), turn(0.5 * a_tail, 1), turn(0.5 * b_tail, 1)]
    r = 1.0 / (e + link + g_end)
    left, right = e * r, link * r
    g = g + left * g_end + turn(right * g_end, 1)
    e = e * right
    levels = []
    by = 1
    while by < n:
        e_left = turn(e, by)
        s = 1.0 / (e_left + e + g)
        lo, hi = e_left * s, e * s
        levels.append((by, lo, hi))
        g = g + turn(lo * g, -by) + turn(hi * g, by)
        e = e * turn(hi, -by)
        by *= 2
    return gain, loss, r, left, right, levels, 1.0 / g


def ring_solve(box, n, ring, order, me, first_out, last_out):
    gain, loss, r, left, right, levels, inv = ring
    size = inv.shape[0]
    for i, which in enumerate(order):
        end = get_row(box, n, 3 + i) + gain[which]
        v = get_row(box, n, i) - loss[which] + left * end + turn(right * end, 1)
        for by, lo, hi in levels:
            v = v + turn(lo * v, -by) + turn(hi * v, by)
        v = v * inv
        first_out[i * size : (i + 1) * size, :] = v
        last_out[i * size : (i + 1) * size, :] = r * end + left * v + right * turn(v, -1)
    return [
        (first_out[pl.ds(i * size + me, 1), :], last_out[pl.ds(i * size + me, 1), :]) for i in range(3)
    ]


def total(x):
    x = jnp.sum(x, axis=0) if x.ndim == 3 else x
    for by in (1, 2, 4):
        x = x + turn(x, by)
    return x[0:1]


def kernel(nx, ny, damping, pot_hbm, lab_hbm, pri_hbm, off_hbm, own_out, first_out, last_out, ends_out, pot, lab, pri, off, box_x, mat_y, box_y,
           labt, ft, first_x, last_x, first_y, last_y, send_x, recv_x, send_y, recv_y, load):
    me_x, me_y = lax.axis_index("gx"), lax.axis_index("gy")
    loads, steps, _, cols = pot.shape
    rows = steps * 8
    for s in range(8):
        pltpu.make_async_copy(lab_hbm.at[pl.ds(s * steps, steps), :], lab.at[:, s, :], load.at[0]).start()
    small = [pltpu.make_async_copy(src, dst, load.at[i]) for i, (src, dst) in enumerate(((pri_hbm, pri), (off_hbm, off)), 1)]
    for copy in small:
        copy.start()
    barrier = pltpu.get_barrier_semaphore()
    for mask in range(1, nx):
        pl.semaphore_signal(barrier, inc=1, device_id={"gx": partner(me_x, mask, nx)}, device_id_type=MESH)
    for mask in range(1, ny):
        pl.semaphore_signal(barrier, inc=1, device_id={"gy": partner(me_y, mask, ny)}, device_id_type=MESH)
    for s in range(8):
        pltpu.make_async_copy(pot_hbm.at[:, pl.ds(s * steps, steps), :], pot.at[:, :, s, :], load.at[3]).start()

    for copy in small:
        copy.wait()
    kx_table, ky_table = 0.5 / spread(pri, 0), 0.5 / spread(pri, 1)
    xy_table, xz_table, yz_table = [spread(off, row) for row in range(3)]
    pltpu.make_async_copy(lab, lab, load.at[0]).wait()
    labels = lab[...]
    k = lookup(kx_table, labels)
    e = faces(k)
    levels, e_in, g, g_end = factor(e, damping)
    a, b = lookup(xy_table, labels), lookup(xz_table, labels)
    source = [e - preceding(e)[0], central(a), central(b)]
    pltpu.make_async_copy(pot, pot, load.at[3]).wait()
    solved = [forward(levels, damping * pot[i] + source[i]) for i in range(3)]
    pl.semaphore_wait(barrier, nx - 1 + ny - 1)
    put_record(box_x, me_x, matrix_rows(e_in, g, g_end, k, a, b) + [s[1][0:1] for s in solved] + [s[2][0:1] for s in solved])
    send_all(box_x, me_x, nx, "gx", send_x.at[1], recv_x.at[1])

    lanes = labt.shape[0] * 128
    repeat = lanes // rows

    def across(q):
        flat = q.reshape(rows, cols)
        if repeat > 1:
            flat = jnp.concatenate([flat] * repeat, 0)
        return flat.T

    def along(q, slot):
        for t in range(ysteps):
            for c in range(lanes // 128):
                ft[slot, c, pl.ds(t, 8, stride=ysteps), :] = q[t, :, c * 128 : (c + 1) * 128]
        return get_wide(ft.at[slot])

    put_wide(labt, across(labels))
    ysteps = cols // 8
    labels_y = strided_wide(labt, ysteps)
    ky, ay, by = [lookup(table, labels_y) for table in (ky_table, xy_table, yz_table)]
    ey = faces(ky)
    levels_y, ey_in, gy, gy_end = factor(ey, damping)
    put_record(mat_y, me_y, matrix_rows(ey_in, gy, gy_end, ky, ay, by))
    send_all(mat_y, me_y, ny, "gy", send_y.at[0], recv_y.at[0])
    source_y = [central(ay), ey - preceding(ey)[0], central(by)]
    base_y = [forward(levels_y, q) for q in source_y]
    zero = jnp.zeros((1, cols), jnp.float32)
    inner = [backward(levels, kept, zero, zero) for kept, _, _ in solved]
    first_part, last_part = homogeneous(levels)
    first_y_part, last_y_part = homogeneous(levels_y)
    first_share, last_share = along(first_y_part, 0), along(last_y_part, 1)
    first_out[...], last_out[...] = first_share, last_share
    first_weight, last_weight = damping * first_share, damping * last_share

    wait_all(mat_y, ny, recv_y.at[0])
    ring_y = ring_factor(mat_y, ny)
    wait_all(box_x, nx, recv_x.at[1])
    ring_x = ring_factor(box_x, nx)
    ends = ring_solve(box_x.at[pl.ds(9, 6)], nx, ring_x, (0, 1, 2), me_x, first_x, last_x)
    turned = [across(inner[i] + first_part * ends[i][0] + last_part * ends[i][1]) for i in range(3)]
    firsts = [base_y[i][1][0:1] + total((first_weight * turned[i]).reshape(ysteps, 8, lanes)) for i in range(3)]
    lasts = [base_y[i][2][0:1] + total((last_weight * turned[i]).reshape(ysteps, 8, lanes)) for i in range(3)]
    put_record(box_y, me_y, firsts + lasts)
    send_all(box_y, me_y, ny, "gy", send_y.at[1], recv_y.at[1])

    row = jnp.zeros((1, lanes), jnp.float32)
    for i in range(3):
        put_wide(ft.at[2 + i], turned[i])
        kept = forward(levels_y, damping * strided_wide(ft.at[2 + i], ysteps) + source_y[i])[0]
        own_out[i] = along(backward(levels_y, kept, row, row), 2 + i).T[:rows].reshape(steps, 8, cols)
    wait_all(box_y, ny, recv_y.at[1])
    ends = ring_solve(box_y, ny, ring_y, (1, 0, 2), me_y, first_y, last_y)
    for i in range(3):
        ends_out[2 * i : 2 * i + 1, :] = ends[i][0]
        ends_out[2 * i + 1 : 2 * i + 2, :] = ends[i][1]
    for box, n, sem in ((box_x, nx, send_x.at[1]), (mat_y, ny, send_y.at[0]), (box_y, ny, send_y.at[1])):
        wait_all(box, n, sem)


def store(own, first, last, ends, out, v, sem):
    loads, steps, _, cols = v.shape
    for i in range(loads):
        change = first[...] * ends[2 * i : 2 * i + 1, :] + last[...] * ends[2 * i + 1 : 2 * i + 2, :]
        v[i] = own[i] + change.T[: steps * 8].reshape(steps, 8, cols)
        for s in range(8):
            pltpu.make_async_copy(v.at[i, :, s, :], out.at[i, pl.ds(s * steps, steps), :], sem).start()
    pltpu.make_async_copy(v, v, sem).wait()


def local(potential, labels, principal, off_diagonal):
    nx, ny = lax.axis_size("gx"), lax.axis_size("gy")
    loads, _, rows, cols = potential.shape
    lanes = max(rows, 128)
    steps = rows // 8
    damping = 2.0 / (cols * cols)
    vmem = pl.BlockSpec(memory_space=pltpu.VMEM)
    hbm = pl.BlockSpec(memory_space=pltpu.HBM)
    args = (potential.reshape(loads, rows, cols), labels.reshape(rows, cols), principal, off_diagonal)
    result = pl.pallas_call(
        functools.partial(kernel, nx, ny, damping),
        out_shape=[
            pltpu.VMEM(shape, jnp.float32)
            for shape in ((loads, steps, 8, cols), (cols, lanes), (cols, lanes), (2 * loads, lanes))
        ],
        in_specs=[hbm] * 4,
        out_specs=[vmem] * 4,
        scratch_shapes=[
            pltpu.VMEM((loads, steps, 8, cols), jnp.float32),
            pltpu.VMEM((steps, 8, cols), jnp.int32),
            pltpu.VMEM(principal.shape, jnp.float32),
            pltpu.VMEM(off_diagonal.shape, jnp.float32),
            pltpu.VMEM((15, nx, cols), jnp.float32),
            pltpu.VMEM((9, ny, lanes), jnp.float32),
            pltpu.VMEM((6, ny, lanes), jnp.float32),
            pltpu.VMEM((lanes // 128, cols, 128), jnp.int32),
            pltpu.VMEM((5, lanes // 128, cols, 128), jnp.float32),
            pltpu.VMEM((loads * max(nx, 8), cols), jnp.float32),
            pltpu.VMEM((loads * max(nx, 8), cols), jnp.float32),
            pltpu.VMEM((loads * max(ny, 8), lanes), jnp.float32),
            pltpu.VMEM((loads * max(ny, 8), lanes), jnp.float32),
            pltpu.SemaphoreType.DMA((2,)),
            pltpu.SemaphoreType.DMA((2,)),
            pltpu.SemaphoreType.DMA((2,)),
            pltpu.SemaphoreType.DMA((2,)),
            pltpu.SemaphoreType.DMA((4,)),
        ],
        compiler_params=pltpu.CompilerParams(
            collective_id=0, has_side_effects=True, vmem_limit_bytes=32 * 1024 * 1024
        ),
    )(*[pltpu.with_memory_space_constraint(x, pltpu.HBM) for x in args])
    result = pl.pallas_call(
        store,
        out_shape=pltpu.HBM((loads, rows, cols), jnp.float32),
        in_specs=[vmem] * 4,
        out_specs=hbm,
        scratch_shapes=[pltpu.VMEM((loads, steps, 8, cols), jnp.float32), pltpu.SemaphoreType.DMA],
        compiler_params=pltpu.CompilerParams(vmem_limit_bytes=8 * 1024 * 1024),
    )(*[pltpu.with_memory_space_constraint(x, pltpu.VMEM) for x in result])
    return result.reshape(potential.shape)


def solution(mesh):
    in_specs = (P(None, None, "gx", "gy"), P(None, "gx", "gy"), P(), P())
    out_specs = P(None, None, "gx", "gy")
    return jax.shard_map(local, mesh=mesh, in_specs=in_specs, out_specs=out_specs, check_vma=False)
```

```python
import functools

import jax
import jax.numpy as jnp
from jax import lax
from jax.experimental import pallas as pl
from jax.experimental.pallas import tpu as pltpu
from jax.sharding import PartitionSpec as P

MESH = pl.DeviceIdType.MESH
ROWS = 8


def sublane(shape):
    return lax.broadcasted_iota(jnp.int32, shape, len(shape) - 2)


def turn(x, by):
    size = x.shape[0]
    by = by % size
    return x if by == 0 else pltpu.roll(x, by, 0)


def following(q, last):
    wrap = turn(q[0], -1)
    wrap = jnp.where(sublane(wrap.shape) == 7, last, wrap)
    return wrap[None] if q.shape[0] == 1 else jnp.concatenate([q[1:], wrap[None]], 0)


def preceding(q):
    wrap = turn(q[-1], 1)
    first = jnp.where(sublane(wrap.shape) == 0, 0.0, wrap)[None]
    return (first if q.shape[0] == 1 else jnp.concatenate([first, q[:-1]], 0)), wrap


def split(q):
    pairs = q.reshape((q.shape[0] // 2, 2) + q.shape[1:])
    return pairs[:, 0], pairs[:, 1]


def merge(even, odd):
    return jnp.stack([even, odd], 1).reshape((2 * even.shape[0],) + even.shape[1:])


def wide(parts):
    return parts[0] if len(parts) == 1 else jnp.concatenate(parts, -1)


def strided(ref, steps):
    return jnp.stack([ref[pl.ds(t, 8, stride=steps), :] for t in range(steps)], 0)


def strided_wide(ref, steps):
    return wide([strided(ref.at[c], steps) for c in range(ref.shape[0])])


def put_wide(ref, value):
    for c in range(ref.shape[0]):
        ref[c] = value[:, c * 128 : (c + 1) * 128]


def get_wide(ref):
    return wide([ref[c] for c in range(ref.shape[0])])


def spread(ref, row):
    lane = lax.broadcasted_iota(jnp.int32, (8, 128), 1)
    out = jnp.full((8, 128), ref[row, 0], jnp.float32)
    for phase in range(1, 8):
        out = jnp.where(lane == phase, ref[row, phase], out)
    return out


def lookup(table, labels):
    width = labels.shape[-1]
    flat = labels.reshape(-1, 8, width)
    out = []
    for t in range(flat.shape[0]):
        parts = [
            jnp.take_along_axis(table, flat[t, :, c : c + 128], axis=1, mode="promise_in_bounds")
            for c in range(0, width, 128)
        ]
        out.append(wide(parts))
    return jnp.stack(out, 0).reshape(labels.shape)


def at_end(q, value):
    end = jnp.where(sublane(q.shape[1:]) == 7, value, q[-1])[None]
    return end if q.shape[0] == 1 else jnp.concatenate([q[:-1], end], 0)


def faces(half_inverse):
    return at_end(1.0 / (half_inverse + following(half_inverse, half_inverse[0])), 0.0)


def factor(e, damping):
    g = jnp.full(e.shape, damping, jnp.float32)
    levels = []
    g_end = jnp.zeros(e.shape[1:], jnp.float32)
    top = True
    while e.shape[0] > 1:
        e_even, e_odd = split(e)
        g_even, g_odd = split(g)
        r = 1.0 / (e_even + e_odd + g_odd)
        if top:
            r = at_end(r, 0.0)
            right = at_end(e_odd * r, 1.0)
        else:
            right = e_odd * r
        left = e_even * r
        top = False
        levels.append((left, right, r))
        e = e_even * right
        moved, wrap = preceding(right * g_odd)
        g = g_even + left * g_odd + moved
        g_end = g_end + wrap
    e, g = e[0], g[0]
    sub = sublane(e.shape)
    for by in (1, 2, 4):
        chosen = sub % (2 * by) == by
        e_left = turn(e, by)
        r = jnp.where(chosen, 1.0 / (e_left + e + g), 0.0)
        left, right = e_left * r, e * r
        levels.append((left, right, r))
        e = e * turn(right, -by)
        wrap = turn(right * g, by)
        g = g + turn(left * g, -by) + jnp.where(sub == 0, 0.0, wrap)
        g_end = g_end + wrap
    return levels, e, g, g_end


def forward(levels, f):
    kept = []
    f_end = jnp.zeros(f.shape[1:], jnp.float32)
    for left, right, r in levels[:-3]:
        f_even, f_odd = split(f)
        kept.append(f_odd)
        moved, wrap = preceding(right * f_odd)
        f = f_even + left * f_odd + moved
        f_end = f_end + wrap
    f = f[0]
    sub = sublane(f.shape)
    for by, (left, right, r) in zip((1, 2, 4), levels[-3:]):
        kept.append(f)
        wrap = turn(right * f, by)
        f = f + turn(left * f, -by) + jnp.where(sub == 0, 0.0, wrap)
        f_end = f_end + wrap
    return kept, f, f_end


def backward(levels, kept, first, last):
    shape = levels[-1][2].shape
    sub = sublane(shape)
    kept = [None] * len(levels) if kept is None else kept
    v = jnp.broadcast_to(first, shape)
    last = jnp.broadcast_to(last, shape)

    def between(level, own, low, high):
        left, right, r = level
        inner = left * low + right * high
        return inner if own is None else own * r + inner

    for by, level, own in zip((4, 2, 1), levels[:-4:-1], kept[:-4:-1]):
        after = jnp.where(sub >= 8 - by, last, turn(v, -by))
        v = jnp.where(sub % (2 * by) == by, between(level, own, turn(v, by), after), v)
    v = v[None]
    for level, own in zip(levels[:-3][::-1], kept[:-3][::-1]):
        v = merge(v, between(level, own, v, following(v, last)))
    return v


def homogeneous(levels):
    row = jnp.zeros_like(levels[-1][2][0:1])
    return backward(levels, None, row + 1.0, row), backward(levels, None, row, row + 1.0)


def central(k):
    return following(k, jnp.zeros_like(k[0])) - preceding(k)[0]


def matrix_rows(e, g, g_end, k, a, b):
    return [e[0:1], g[0:1], g_end[0:1]] + [q for x in (k, a, b) for q in (x[0, 0:1], x[-1, 7:8])]


def put_record(box, me, rows):
    for q, row in enumerate(rows):
        box[q, pl.ds(me, 1), :] = row


def partner(me, mask, n):
    if n & (n - 1):
        return lax.rem(me + mask, n)
    out = me
    bit = 1
    while bit < n:
        if mask & bit:
            out = out + bit * (1 - 2 * lax.rem(lax.div(me, bit), 2))
        bit *= 2
    return out


def send_all(box, me, n, axis, send, recv):
    slot = box.at[:, pl.ds(me, 1), :]
    for k in range(n - 1):
        pltpu.make_async_remote_copy(
            src_ref=slot,
            dst_ref=slot,
            send_sem=send,
            recv_sem=recv,
            device_id={axis: k + lax.div(k - me + n, n)},
            device_id_type=MESH,
        ).start()


def wait_all(box, n, sem):
    rest = box.at[:, pl.ds(0, n - 1), :]
    pltpu.make_async_copy(rest, rest, sem).wait()


def get_row(box, n, q):
    if n >= 8:
        return box[q]
    width = box.shape[-1]
    sub = sublane((8, width)) % n
    out = jnp.broadcast_to(box[q, 0:1, :], (8, width))
    for i in range(1, n):
        out = jnp.where(sub == i, jnp.broadcast_to(box[q, i : i + 1, :], (8, width)), out)
    return out


def ring_factor(box, n):
    e, g, g_end, k_head, k_tail, a_head, a_tail, b_head, b_tail = [get_row(box, n, q) for q in range(9)]
    series = k_tail + turn(k_head, -1)
    link = 1.0 / series
    gain = [link, turn(a_head, -1), turn(b_head, -1)]
    loss = [turn(link, 1), turn(a_tail, 1), turn(b_tail, 1)]
    right = 1.0 / (series * (e + g_end) + 1.0)
    r = series * right
    left = e * r
    g = g + left * g_end + turn(right * g_end, 1)
    e = e * right
    levels = []
    by = 1
    while by < n:
        e_left = turn(e, by)
        s = 1.0 / (e_left + e + g)
        lo, hi = e_left * s, e * s
        levels.append((by, lo, hi))
        g = g + turn(lo * g, -by) + turn(hi * g, by)
        e = e * turn(hi, -by)
        by *= 2
    return gain, loss, r, left, right, levels, 1.0 / g


def ring_solve(box, n, ring, order, me, first_out, last_out):
    gain, loss, r, left, right, levels, inv = ring
    size = inv.shape[0]
    for i, which in enumerate(order):
        end = get_row(box, n, 3 + i) + gain[which]
        v = get_row(box, n, i) - loss[which] + left * end + turn(right * end, 1)
        for by, lo, hi in levels:
            v = v + turn(lo * v, -by) + turn(hi * v, by)
        v = v * inv
        first_out[i * size : (i + 1) * size, :] = v
        last_out[i * size : (i + 1) * size, :] = r * end + left * v + right * turn(v, -1)
    return [
        (first_out[pl.ds(i * size + me, 1), :], last_out[pl.ds(i * size + me, 1), :]) for i in range(3)
    ]


def stacked(rows):
    shape = (8, rows[0].shape[1])
    out = jnp.zeros(shape, jnp.float32)
    for i, row in enumerate(rows):
        out = jnp.where(sublane(shape) == i, row, out)
    return out


def total(x):
    x = jnp.sum(x, axis=0) if x.ndim == 3 else x
    for by in (1, 2, 4):
        x = x + turn(x, by)
    return x[0:1]


def kernel(nx, ny, damping, pot_hbm, lab_hbm, pri_hbm, off_hbm, own_out, first_out, last_out, ends_out, pot, lab, pri, off, box_x, mat_y, box_y,
           labt, ft, first_x, last_x, first_y, last_y, send_x, recv_x, send_y, recv_y, load):
    me_x, me_y = lax.axis_index("gx"), lax.axis_index("gy")
    loads, steps, _, cols = pot.shape
    rows = steps * 8
    small = [pltpu.make_async_copy(src, dst, load.at[i]) for i, (src, dst) in enumerate(((pri_hbm, pri), (off_hbm, off)), 1)]
    for copy in small:
        copy.start()
    for s in range(8):
        pltpu.make_async_copy(lab_hbm.at[pl.ds(s * steps, steps), :], lab.at[:, s, :], load.at[0]).start()
    barrier = pltpu.get_barrier_semaphore()
    for mask in range(nx - 1, 0, -1):
        pl.semaphore_signal(barrier, inc=1, device_id={"gx": partner(me_x, mask, nx)}, device_id_type=MESH)
    for mask in range(1, ny):
        pl.semaphore_signal(barrier, inc=1, device_id={"gy": partner(me_y, mask, ny)}, device_id_type=MESH)
    for s in range(8):
        pltpu.make_async_copy(pot_hbm.at[:, pl.ds(s * steps, steps), :], pot.at[:, :, s, :], load.at[3]).start()

    for copy in small:
        copy.wait()
    kx_table, ky_table = 0.5 / spread(pri, 0), 0.5 / spread(pri, 1)
    xy_table, xz_table, yz_table = [0.5 * spread(off, row) for row in range(3)]
    pltpu.make_async_copy(lab, lab, load.at[0]).wait()
    labels = lab[...]
    k = lookup(kx_table, labels)
    e = faces(k)
    pltpu.make_async_copy(pot, pot, load.at[3]).wait()
    levels, e_in, g, g_end = factor(e, damping)
    a, b = lookup(xy_table, labels), lookup(xz_table, labels)
    source = [e - preceding(e)[0], central(a), central(b)]
    solved = [forward(levels, damping * pot[i] + source[i]) for i in range(3)]
    put_record(box_x, me_x, matrix_rows(e_in, g, g_end, k, a, b) + [s[1][0:1] for s in solved] + [s[2][0:1] for s in solved])
    pl.semaphore_wait(barrier, nx - 1 + ny - 1)
    send_all(box_x, me_x, nx, "gx", send_x.at[0], recv_x.at[0])

    lanes = labt.shape[0] * 128
    repeat = lanes // rows

    def across(q):
        flat = q.reshape(rows, cols)
        if repeat > 1:
            flat = jnp.concatenate([flat] * repeat, 0)
        return flat.T

    def along(q, slot):
        for t in range(ysteps):
            for c in range(lanes // 128):
                ft[slot, c, pl.ds(t, 8, stride=ysteps), :] = q[t, :, c * 128 : (c + 1) * 128]
        return get_wide(ft.at[slot])

    put_wide(labt, across(labels))
    ysteps = cols // 8
    labels_y = strided_wide(labt, ysteps)
    ky, ay, by = [lookup(table, labels_y) for table in (ky_table, xy_table, yz_table)]
    ey = faces(ky)
    levels_y, ey_in, gy, gy_end = factor(ey, damping)
    put_record(mat_y, me_y, matrix_rows(ey_in, gy, gy_end, ky, ay, by))
    send_all(mat_y, me_y, ny, "gy", send_y.at[0], recv_y.at[0])
    source_y = [central(ay), ey - preceding(ey)[0], central(by)]
    base_y = [forward(levels_y, q) for q in source_y]
    zero = jnp.zeros((1, cols), jnp.float32)
    inner = [backward(levels, kept, zero, zero) for kept, _, _ in solved]
    first_part, last_part = homogeneous(levels)
    first_y_part, last_y_part = homogeneous(levels_y)
    first_share, last_share = along(first_y_part, 0), along(last_y_part, 1)
    first_out[...], last_out[...] = first_share, last_share
    first_weight, last_weight = damping * first_share, damping * last_share
    turned = [across(q) for q in inner]
    base_firsts = [base_y[i][1][0:1] + total((first_weight * turned[i]).reshape(ysteps, 8, lanes)) for i in range(3)]
    base_lasts = [base_y[i][2][0:1] + total((last_weight * turned[i]).reshape(ysteps, 8, lanes)) for i in range(3)]
    parts = [across(first_part), across(last_part)]
    response = jnp.concatenate([jnp.concatenate([w * q for w in (first_weight, last_weight)], 1) for q in parts], 0)
    response_hi = response.astype(jnp.bfloat16)
    response_lo = (response - response_hi.astype(jnp.float32)).astype(jnp.bfloat16)

    wait_all(mat_y, ny, recv_y.at[0])
    ring_y = ring_factor(mat_y, ny)
    wait_all(box_x, nx, recv_x.at[0])
    ring_x = ring_factor(box_x, nx)
    ends = ring_solve(box_x.at[pl.ds(9, 6)], nx, ring_x, (0, 1, 2), me_x, first_x, last_x)
    vector = jnp.concatenate([stacked([ends[i][0] for i in range(3)]), stacked([ends[i][1] for i in range(3)])], 1)
    coarse = vector.astype(jnp.bfloat16).astype(jnp.float32)
    operand = jnp.concatenate([coarse, vector - coarse], 0).astype(jnp.bfloat16)
    response = jnp.dot(operand, response_hi, preferred_element_type=jnp.float32)
    response = response[:8] + response[8:] + jnp.dot(operand, response_lo, preferred_element_type=jnp.float32)[:8]
    firsts = [base_firsts[i] + response[i : i + 1, :lanes] for i in range(3)]
    lasts = [base_lasts[i] + response[i : i + 1, lanes:] for i in range(3)]
    put_record(box_y, me_y, firsts + lasts)
    send_all(box_y, me_y, ny, "gy", send_y.at[1], recv_y.at[1])

    row = jnp.zeros((1, lanes), jnp.float32)
    for i in range(3):
        put_wide(ft.at[2 + i], turned[i] + across(first_part * ends[i][0] + last_part * ends[i][1]))
        kept = forward(levels_y, damping * strided_wide(ft.at[2 + i], ysteps) + source_y[i])[0]
        own_out[i] = along(backward(levels_y, kept, row, row), 2 + i).T[:rows].reshape(steps, 8, cols)
    wait_all(box_y, ny, recv_y.at[1])
    ends = ring_solve(box_y, ny, ring_y, (1, 0, 2), me_y, first_y, last_y)
    for i in range(3):
        ends_out[2 * i : 2 * i + 1, :] = ends[i][0]
        ends_out[2 * i + 1 : 2 * i + 2, :] = ends[i][1]
    for box, n, sem in ((box_x, nx, send_x.at[0]), (mat_y, ny, send_y.at[0]), (box_y, ny, send_y.at[1])):
        wait_all(box, n, sem)


def store(own, first, last, ends, out, v, sem):
    loads, steps, _, cols = v.shape
    for i in range(loads):
        change = first[...] * ends[2 * i : 2 * i + 1, :] + last[...] * ends[2 * i + 1 : 2 * i + 2, :]
        v[i] = own[i] + change.T[: steps * 8].reshape(steps, 8, cols)
        for s in range(8):
            pltpu.make_async_copy(v.at[i, :, s, :], out.at[i, pl.ds(s * steps, steps), :], sem).start()
    pltpu.make_async_copy(v, v, sem).wait()


def local(potential, labels, principal, off_diagonal):
    nx, ny = lax.axis_size("gx"), lax.axis_size("gy")
    loads, _, rows, cols = potential.shape
    lanes = max(rows, 128)
    steps = rows // 8
    damping = 2.0 / (cols * cols)
    vmem = pl.BlockSpec(memory_space=pltpu.VMEM)
    hbm = pl.BlockSpec(memory_space=pltpu.HBM)
    args = (potential.reshape(loads, rows, cols), labels.reshape(rows, cols), principal, off_diagonal)
    result = pl.pallas_call(
        functools.partial(kernel, nx, ny, damping),
        out_shape=[
            pltpu.VMEM(shape, jnp.float32)
            for shape in ((loads, steps, 8, cols), (cols, lanes), (cols, lanes), (2 * loads, lanes))
        ],
        in_specs=[hbm] * 4,
        out_specs=[vmem] * 4,
        scratch_shapes=[
            pltpu.VMEM((loads, steps, 8, cols), jnp.float32),
            pltpu.VMEM((steps, 8, cols), jnp.int32),
            pltpu.SMEM(principal.shape, jnp.float32),
            pltpu.SMEM(off_diagonal.shape, jnp.float32),
            pltpu.VMEM((15, nx, cols), jnp.float32),
            pltpu.VMEM((9, ny, lanes), jnp.float32),
            pltpu.VMEM((6, ny, lanes), jnp.float32),
            pltpu.VMEM((lanes // 128, cols, 128), jnp.int32),
            pltpu.VMEM((5, lanes // 128, cols, 128), jnp.float32),
            pltpu.VMEM((loads * max(nx, 8), cols), jnp.float32),
            pltpu.VMEM((loads * max(nx, 8), cols), jnp.float32),
            pltpu.VMEM((loads * max(ny, 8), lanes), jnp.float32),
            pltpu.VMEM((loads * max(ny, 8), lanes), jnp.float32),
            pltpu.SemaphoreType.DMA((1,)),
            pltpu.SemaphoreType.DMA((1,)),
            pltpu.SemaphoreType.DMA((2,)),
            pltpu.SemaphoreType.DMA((2,)),
            pltpu.SemaphoreType.DMA((4,)),
        ],
        compiler_params=pltpu.CompilerParams(
            collective_id=0, has_side_effects=True, vmem_limit_bytes=32 * 1024 * 1024
        ),
    )(*[pltpu.with_memory_space_constraint(x, pltpu.HBM) for x in args])
    result = pl.pallas_call(
        store,
        out_shape=pltpu.HBM((loads, rows, cols), jnp.float32),
        in_specs=[vmem] * 4,
        out_specs=hbm,
        scratch_shapes=[pltpu.VMEM((loads, steps, 8, cols), jnp.float32), pltpu.SemaphoreType.DMA],
        compiler_params=pltpu.CompilerParams(vmem_limit_bytes=8 * 1024 * 1024),
    )(*[pltpu.with_memory_space_constraint(x, pltpu.VMEM) for x in result])
    return result.reshape(potential.shape)


def solution(mesh):
    in_specs = (P(None, None, "gx", "gy"), P(None, "gx", "gy"), P(), P())
    out_specs = P(None, None, "gx", "gy")
    return jax.shard_map(local, mesh=mesh, in_specs=in_specs, out_specs=out_specs, check_vma=False)
```

```python
import functools

import jax
import jax.numpy as jnp
from jax import lax
from jax.experimental import pallas as pl
from jax.experimental.pallas import tpu as pltpu
from jax.sharding import PartitionSpec as P

MESH = pl.DeviceIdType.MESH
ROWS = 8


def sublane(shape):
    return lax.broadcasted_iota(jnp.int32, shape, len(shape) - 2)


def turn(x, by):
    size = x.shape[0]
    by = by % size
    return x if by == 0 else pltpu.roll(x, by, 0)


def following(q, last):
    wrap = turn(q[0], -1)
    wrap = jnp.where(sublane(wrap.shape) == 7, last, wrap)
    return wrap[None] if q.shape[0] == 1 else jnp.concatenate([q[1:], wrap[None]], 0)


def preceding(q):
    wrap = turn(q[-1], 1)
    first = jnp.where(sublane(wrap.shape) == 0, 0.0, wrap)[None]
    return (first if q.shape[0] == 1 else jnp.concatenate([first, q[:-1]], 0)), wrap


def split(q):
    pairs = q.reshape((q.shape[0] // 2, 2) + q.shape[1:])
    return pairs[:, 0], pairs[:, 1]


def merge(even, odd):
    return jnp.stack([even, odd], 1).reshape((2 * even.shape[0],) + even.shape[1:])


def wide(parts):
    return parts[0] if len(parts) == 1 else jnp.concatenate(parts, -1)


def strided(ref, steps):
    return jnp.stack([ref[pl.ds(t, 8, stride=steps), :] for t in range(steps)], 0)


def strided_wide(ref, steps):
    return wide([strided(ref.at[c], steps) for c in range(ref.shape[0])])


def put_wide(ref, value):
    for c in range(ref.shape[0]):
        ref[c] = value[:, c * 128 : (c + 1) * 128]


def get_wide(ref):
    return wide([ref[c] for c in range(ref.shape[0])])


def spread(ref, row):
    lane = lax.broadcasted_iota(jnp.int32, (8, 128), 1)
    out = jnp.full((8, 128), ref[row, 0], jnp.float32)
    for phase in range(1, 8):
        out = jnp.where(lane == phase, ref[row, phase], out)
    return out


def lookup(table, labels):
    width = labels.shape[-1]
    flat = labels.reshape(-1, 8, width)
    out = []
    for t in range(flat.shape[0]):
        parts = [
            jnp.take_along_axis(table, flat[t, :, c : c + 128], axis=1, mode="promise_in_bounds")
            for c in range(0, width, 128)
        ]
        out.append(wide(parts))
    return jnp.stack(out, 0).reshape(labels.shape)


def at_end(q, value):
    end = jnp.where(sublane(q.shape[1:]) == 7, value, q[-1])[None]
    return end if q.shape[0] == 1 else jnp.concatenate([q[:-1], end], 0)


def faces(half_inverse):
    return at_end(1.0 / (half_inverse + following(half_inverse, half_inverse[0])), 0.0)


def factor(e, damping):
    g = jnp.full(e.shape, damping, jnp.float32)
    levels = []
    g_end = jnp.zeros(e.shape[1:], jnp.float32)
    top = True
    while e.shape[0] > 1:
        e_even, e_odd = split(e)
        g_even, g_odd = split(g)
        r = 1.0 / (e_even + e_odd + g_odd)
        if top:
            r = at_end(r, 0.0)
            right = at_end(e_odd * r, 1.0)
        else:
            right = e_odd * r
        left = e_even * r
        top = False
        levels.append((left, right, r))
        e = e_even * right
        moved, wrap = preceding(right * g_odd)
        g = g_even + left * g_odd + moved
        g_end = g_end + wrap
    e, g = e[0], g[0]
    sub = sublane(e.shape)
    for by in (1, 2, 4):
        chosen = sub % (2 * by) == by
        e_left = turn(e, by)
        r = jnp.where(chosen, 1.0 / (e_left + e + g), 0.0)
        left, right = e_left * r, e * r
        levels.append((left, right, r))
        e = e * turn(right, -by)
        wrap = turn(right * g, by)
        g = g + turn(left * g, -by) + jnp.where(sub == 0, 0.0, wrap)
        g_end = g_end + wrap
    return levels, e, g, g_end


def forward(levels, f):
    kept = []
    f_end = jnp.zeros(f.shape[1:], jnp.float32)
    for left, right, r in levels[:-3]:
        f_even, f_odd = split(f)
        kept.append(f_odd)
        moved, wrap = preceding(right * f_odd)
        f = f_even + left * f_odd + moved
        f_end = f_end + wrap
    f = f[0]
    sub = sublane(f.shape)
    for by, (left, right, r) in zip((1, 2, 4), levels[-3:]):
        kept.append(f)
        wrap = turn(right * f, by)
        f = f + turn(left * f, -by) + jnp.where(sub == 0, 0.0, wrap)
        f_end = f_end + wrap
    return kept, f, f_end


def backward(levels, kept, first, last):
    shape = levels[-1][2].shape
    sub = sublane(shape)
    kept = [None] * len(levels) if kept is None else kept
    v = jnp.broadcast_to(first, shape)
    last = jnp.broadcast_to(last, shape)

    def between(level, own, low, high):
        left, right, r = level
        inner = left * low + right * high
        return inner if own is None else own * r + inner

    for by, level, own in zip((4, 2, 1), levels[:-4:-1], kept[:-4:-1]):
        after = jnp.where(sub >= 8 - by, last, turn(v, -by))
        v = jnp.where(sub % (2 * by) == by, between(level, own, turn(v, by), after), v)
    v = v[None]
    for level, own in zip(levels[:-3][::-1], kept[:-3][::-1]):
        v = merge(v, between(level, own, v, following(v, last)))
    return v


def homogeneous(levels):
    row = jnp.zeros_like(levels[-1][2][0:1])
    return backward(levels, None, row + 1.0, row), backward(levels, None, row, row + 1.0)


def central(k):
    return following(k, jnp.zeros_like(k[0])) - preceding(k)[0]


def matrix_rows(e, g, g_end, k, a, b):
    return [e[0:1], g[0:1], g_end[0:1]] + [q for x in (k, a, b) for q in (x[0, 0:1], x[-1, 7:8])]


def put_record(box, me, rows):
    for q, row in enumerate(rows):
        box[q, pl.ds(me, 1), :] = row


def partner(me, mask, n):
    if n & (n - 1):
        return lax.rem(me + mask, n)
    out = me
    bit = 1
    while bit < n:
        if mask & bit:
            out = out + bit * (1 - 2 * lax.rem(lax.div(me, bit), 2))
        bit *= 2
    return out


def send_all(box, me, n, axis, send, recv, begin=0, end=None):
    slot = box.at[:, pl.ds(me, 1), :]
    for k in range(begin, n - 1 if end is None else end):
        pltpu.make_async_remote_copy(
            src_ref=slot,
            dst_ref=slot,
            send_sem=send,
            recv_sem=recv,
            device_id={axis: k + lax.div(k - me + n, n)},
            device_id_type=MESH,
        ).start()


def wait_all(box, n, sem):
    rest = box.at[:, pl.ds(0, n - 1), :]
    pltpu.make_async_copy(rest, rest, sem).wait()


def get_row(box, n, q):
    if n >= 8:
        return box[q]
    width = box.shape[-1]
    sub = sublane((8, width)) % n
    out = jnp.broadcast_to(box[q, 0:1, :], (8, width))
    for i in range(1, n):
        out = jnp.where(sub == i, jnp.broadcast_to(box[q, i : i + 1, :], (8, width)), out)
    return out


def ring_factor(box, n):
    e, g, g_end, k_head, k_tail, a_head, a_tail, b_head, b_tail = [get_row(box, n, q) for q in range(9)]
    series = k_tail + turn(k_head, -1)
    link = 1.0 / series
    gain = [link, turn(a_head, -1), turn(b_head, -1)]
    loss = [turn(link, 1), turn(a_tail, 1), turn(b_tail, 1)]
    right = 1.0 / (series * (e + g_end) + 1.0)
    r = series * right
    left = e * r
    g = g + left * g_end + turn(right * g_end, 1)
    e = e * right
    levels = []
    by = 1
    while by < n:
        e_left = turn(e, by)
        s = 1.0 / (e_left + e + g)
        lo, hi = e_left * s, e * s
        levels.append((by, lo, hi))
        g = g + turn(lo * g, -by) + turn(hi * g, by)
        e = e * turn(hi, -by)
        by *= 2
    return gain, loss, r, left, right, levels, 1.0 / g


def ring_solve(box, n, ring, order, me, first_out, last_out):
    gain, loss, r, left, right, levels, inv = ring
    size = inv.shape[0]
    for i, which in enumerate(order):
        end = get_row(box, n, 3 + i) + gain[which]
        v = get_row(box, n, i) - loss[which] + left * end + turn(right * end, 1)
        for by, lo, hi in levels:
            v = v + turn(lo * v, -by) + turn(hi * v, by)
        v = v * inv
        first_out[i * size : (i + 1) * size, :] = v
        last_out[i * size : (i + 1) * size, :] = r * end + left * v + right * turn(v, -1)
    return [
        (first_out[pl.ds(i * size + me, 1), :], last_out[pl.ds(i * size + me, 1), :]) for i in range(3)
    ]


def stacked(rows):
    shape = (8, rows[0].shape[1])
    out = jnp.zeros(shape, jnp.float32)
    for i, row in enumerate(rows):
        out = jnp.where(sublane(shape) == i, row, out)
    return out


def total(x):
    x = jnp.sum(x, axis=0) if x.ndim == 3 else x
    for by in (1, 2, 4):
        x = x + turn(x, by)
    return x[0:1]


def kernel(nx, ny, damping, pot_hbm, lab_hbm, pri_hbm, off_hbm, own_out, first_out, last_out, ends_out, pot, lab, pri, off, box_x, mat_y, box_y,
           labt, ft, first_x, last_x, first_y, last_y, send_x, recv_x, send_y, recv_y, load):
    me_x, me_y = lax.axis_index("gx"), lax.axis_index("gy")
    loads, steps, _, cols = pot.shape
    rows = steps * 8
    small = [pltpu.make_async_copy(src, dst, load.at[i]) for i, (src, dst) in enumerate(((pri_hbm, pri), (off_hbm, off)), 1)]
    for copy in small:
        copy.start()
    for s in range(8):
        pltpu.make_async_copy(lab_hbm.at[pl.ds(s * steps, steps), :], lab.at[:, s, :], load.at[0]).start()
    barrier = pltpu.get_barrier_semaphore()
    for mask in range(nx - 1, 0, -1):
        pl.semaphore_signal(barrier, inc=1, device_id={"gx": partner(me_x, mask, nx)}, device_id_type=MESH)
    for mask in range(1, ny):
        pl.semaphore_signal(barrier, inc=1, device_id={"gy": partner(me_y, mask, ny)}, device_id_type=MESH)
    for s in range(8):
        pltpu.make_async_copy(pot_hbm.at[:, pl.ds(s * steps, steps), :], pot.at[:, :, s, :], load.at[3]).start()

    for copy in small:
        copy.wait()
    kx_table, ky_table = 0.5 / spread(pri, 0), 0.5 / spread(pri, 1)
    xy_table, xz_table, yz_table = [0.5 * spread(off, row) for row in range(3)]
    pltpu.make_async_copy(lab, lab, load.at[0]).wait()
    labels = lab[...]
    k = lookup(kx_table, labels)
    e = faces(k)
    pltpu.make_async_copy(pot, pot, load.at[3]).wait()
    levels, e_in, g, g_end = factor(e, damping)
    a, b = lookup(xy_table, labels), lookup(xz_table, labels)
    source = [e - preceding(e)[0], central(a), central(b)]
    solved = [forward(levels, damping * pot[i] + source[i]) for i in range(3)]
    put_record(box_x, me_x, matrix_rows(e_in, g, g_end, k, a, b) + [s[1][0:1] for s in solved] + [s[2][0:1] for s in solved])
    pl.semaphore_wait(barrier, nx - 1 + ny - 1)
    send_all(box_x, me_x, nx, "gx", send_x.at[0], recv_x.at[0], 0, 4)

    lanes = labt.shape[0] * 128
    repeat = lanes // rows

    def across(q):
        flat = q.reshape(rows, cols)
        if repeat > 1:
            flat = jnp.concatenate([flat] * repeat, 0)
        return flat.T

    def along(q, slot):
        for t in range(ysteps):
            for c in range(lanes // 128):
                ft[slot, c, pl.ds(t, 8, stride=ysteps), :] = q[t, :, c * 128 : (c + 1) * 128]
        return get_wide(ft.at[slot])

    put_wide(labt, across(labels))
    ysteps = cols // 8
    labels_y = strided_wide(labt, ysteps)
    ky, ay, by = [lookup(table, labels_y) for table in (ky_table, xy_table, yz_table)]
    ey = faces(ky)
    levels_y, ey_in, gy, gy_end = factor(ey, damping)
    put_record(mat_y, me_y, matrix_rows(ey_in, gy, gy_end, ky, ay, by))
    send_all(box_x, me_x, nx, "gx", send_x.at[0], recv_x.at[0], 4)
    send_all(mat_y, me_y, ny, "gy", send_y.at[0], recv_y.at[0])
    source_y = [central(ay), ey - preceding(ey)[0], central(by)]
    base_y = [forward(levels_y, q) for q in source_y]
    zero = jnp.zeros((1, cols), jnp.float32)
    inner = [backward(levels, kept, zero, zero) for kept, _, _ in solved]
    first_part, last_part = homogeneous(levels)
    first_y_part, last_y_part = homogeneous(levels_y)
    first_share, last_share = along(first_y_part, 0), along(last_y_part, 1)
    first_out[...], last_out[...] = first_share, last_share
    first_weight, last_weight = damping * first_share, damping * last_share
    turned = [across(q) for q in inner]
    base_firsts = [base_y[i][1][0:1] + total((first_weight * turned[i]).reshape(ysteps, 8, lanes)) for i in range(3)]
    base_lasts = [base_y[i][2][0:1] + total((last_weight * turned[i]).reshape(ysteps, 8, lanes)) for i in range(3)]
    parts = [across(first_part), across(last_part)]
    response = jnp.concatenate([jnp.concatenate([w * q for w in (first_weight, last_weight)], 1) for q in parts], 0)
    response_hi = response.astype(jnp.bfloat16)
    response_lo = (response - response_hi.astype(jnp.float32)).astype(jnp.bfloat16)

    wait_all(mat_y, ny, recv_y.at[0])
    ring_y = ring_factor(mat_y, ny)
    wait_all(box_x, nx, recv_x.at[0])
    ring_x = ring_factor(box_x, nx)
    ends = ring_solve(box_x.at[pl.ds(9, 6)], nx, ring_x, (0, 1, 2), me_x, first_x, last_x)
    vector = jnp.concatenate([stacked([ends[i][0] for i in range(3)]), stacked([ends[i][1] for i in range(3)])], 1)
    coarse = vector.astype(jnp.bfloat16).astype(jnp.float32)
    operand = jnp.concatenate([coarse, vector - coarse], 0).astype(jnp.bfloat16)
    response = jnp.dot(operand, response_hi, preferred_element_type=jnp.float32)
    response = response[:8] + response[8:] + jnp.dot(operand, response_lo, preferred_element_type=jnp.float32)[:8]
    firsts = [base_firsts[i] + response[i : i + 1, :lanes] for i in range(3)]
    lasts = [base_lasts[i] + response[i : i + 1, lanes:] for i in range(3)]
    put_record(box_y, me_y, firsts + lasts)
    send_all(box_y, me_y, ny, "gy", send_y.at[1], recv_y.at[1])

    row = jnp.zeros((1, lanes), jnp.float32)
    for i in range(3):
        put_wide(ft.at[2 + i], turned[i] + across(first_part * ends[i][0] + last_part * ends[i][1]))
        kept = forward(levels_y, damping * strided_wide(ft.at[2 + i], ysteps) + source_y[i])[0]
        own_out[i] = along(backward(levels_y, kept, row, row), 2 + i).T[:rows].reshape(steps, 8, cols)
    wait_all(box_y, ny, recv_y.at[1])
    ends = ring_solve(box_y, ny, ring_y, (1, 0, 2), me_y, first_y, last_y)
    for i in range(3):
        ends_out[2 * i : 2 * i + 1, :] = ends[i][0]
        ends_out[2 * i + 1 : 2 * i + 2, :] = ends[i][1]
    for box, n, sem in ((box_x, nx, send_x.at[0]), (mat_y, ny, send_y.at[0]), (box_y, ny, send_y.at[1])):
        wait_all(box, n, sem)


def store(own, first, last, ends, out, v, sem):
    loads, steps, _, cols = v.shape
    for i in range(loads):
        change = first[...] * ends[2 * i : 2 * i + 1, :] + last[...] * ends[2 * i + 1 : 2 * i + 2, :]
        v[i] = own[i] + change.T[: steps * 8].reshape(steps, 8, cols)
        for s in range(8):
            pltpu.make_async_copy(v.at[i, :, s, :], out.at[i, pl.ds(s * steps, steps), :], sem).start()
    pltpu.make_async_copy(v, v, sem).wait()


def local(potential, labels, principal, off_diagonal):
    nx, ny = lax.axis_size("gx"), lax.axis_size("gy")
    loads, _, rows, cols = potential.shape
    lanes = max(rows, 128)
    steps = rows // 8
    damping = 2.0 / (cols * cols)
    vmem = pl.BlockSpec(memory_space=pltpu.VMEM)
    hbm = pl.BlockSpec(memory_space=pltpu.HBM)
    args = (potential.reshape(loads, rows, cols), labels.reshape(rows, cols), principal, off_diagonal)
    result = pl.pallas_call(
        functools.partial(kernel, nx, ny, damping),
        out_shape=[
            pltpu.VMEM(shape, jnp.float32)
            for shape in ((loads, steps, 8, cols), (cols, lanes), (cols, lanes), (2 * loads, lanes))
        ],
        in_specs=[hbm] * 4,
        out_specs=[vmem] * 4,
        scratch_shapes=[
            pltpu.VMEM((loads, steps, 8, cols), jnp.float32),
            pltpu.VMEM((steps, 8, cols), jnp.int32),
            pltpu.SMEM(principal.shape, jnp.float32),
            pltpu.SMEM(off_diagonal.shape, jnp.float32),
            pltpu.VMEM((15, nx, cols), jnp.float32),
            pltpu.VMEM((9, ny, lanes), jnp.float32),
            pltpu.VMEM((6, ny, lanes), jnp.float32),
            pltpu.VMEM((lanes // 128, cols, 128), jnp.int32),
            pltpu.VMEM((5, lanes // 128, cols, 128), jnp.float32),
            pltpu.VMEM((loads * max(nx, 8), cols), jnp.float32),
            pltpu.VMEM((loads * max(nx, 8), cols), jnp.float32),
            pltpu.VMEM((loads * max(ny, 8), lanes), jnp.float32),
            pltpu.VMEM((loads * max(ny, 8), lanes), jnp.float32),
            pltpu.SemaphoreType.DMA((1,)),
            pltpu.SemaphoreType.DMA((1,)),
            pltpu.SemaphoreType.DMA((2,)),
            pltpu.SemaphoreType.DMA((2,)),
            pltpu.SemaphoreType.DMA((4,)),
        ],
        compiler_params=pltpu.CompilerParams(
            collective_id=0, has_side_effects=True, vmem_limit_bytes=32 * 1024 * 1024
        ),
    )(*[pltpu.with_memory_space_constraint(x, pltpu.HBM) for x in args])
    result = pl.pallas_call(
        store,
        out_shape=pltpu.HBM((loads, rows, cols), jnp.float32),
        in_specs=[vmem] * 4,
        out_specs=hbm,
        scratch_shapes=[pltpu.VMEM((loads, steps, 8, cols), jnp.float32), pltpu.SemaphoreType.DMA],
        compiler_params=pltpu.CompilerParams(vmem_limit_bytes=8 * 1024 * 1024),
    )(*[pltpu.with_memory_space_constraint(x, pltpu.VMEM) for x in result])
    return result.reshape(potential.shape)


def solution(mesh):
    in_specs = (P(None, None, "gx", "gy"), P(None, "gx", "gy"), P(), P())
    out_specs = P(None, None, "gx", "gy")
    return jax.shard_map(local, mesh=mesh, in_specs=in_specs, out_specs=out_specs, check_vma=False)
```

```python
import functools

import jax
import jax.numpy as jnp
from jax import lax
from jax.experimental import pallas as pl
from jax.experimental.pallas import tpu as pltpu
from jax.sharding import PartitionSpec as P

MESH = pl.DeviceIdType.MESH
ROWS = 8


def sublane(shape):
    return lax.broadcasted_iota(jnp.int32, shape, len(shape) - 2)


def turn(x, by):
    size = x.shape[0]
    by = by % size
    return x if by == 0 else pltpu.roll(x, by, 0)


def following(q, last):
    wrap = turn(q[0], -1)
    wrap = jnp.where(sublane(wrap.shape) == 7, last, wrap)
    return wrap[None] if q.shape[0] == 1 else jnp.concatenate([q[1:], wrap[None]], 0)


def preceding(q):
    wrap = turn(q[-1], 1)
    first = jnp.where(sublane(wrap.shape) == 0, 0.0, wrap)[None]
    return (first if q.shape[0] == 1 else jnp.concatenate([first, q[:-1]], 0)), wrap


def split(q):
    pairs = q.reshape((q.shape[0] // 2, 2) + q.shape[1:])
    return pairs[:, 0], pairs[:, 1]


def merge(even, odd):
    return jnp.stack([even, odd], 1).reshape((2 * even.shape[0],) + even.shape[1:])


def wide(parts):
    return parts[0] if len(parts) == 1 else jnp.concatenate(parts, -1)


def strided(ref, steps):
    return jnp.stack([ref[pl.ds(t, 8, stride=steps), :] for t in range(steps)], 0)


def strided_wide(ref, steps):
    return wide([strided(ref.at[c], steps) for c in range(ref.shape[0])])


def put_wide(ref, value):
    for c in range(ref.shape[0]):
        ref[c] = value[:, c * 128 : (c + 1) * 128]


def get_wide(ref):
    return wide([ref[c] for c in range(ref.shape[0])])


def spread(ref, row):
    lane = lax.broadcasted_iota(jnp.int32, (8, 128), 1)
    out = jnp.full((8, 128), ref[row, 0], jnp.float32)
    for phase in range(1, 8):
        out = jnp.where(lane == phase, ref[row, phase], out)
    return out


def lookup(table, labels):
    width = labels.shape[-1]
    flat = labels.reshape(-1, 8, width)
    out = []
    for t in range(flat.shape[0]):
        parts = [
            jnp.take_along_axis(table, flat[t, :, c : c + 128], axis=1, mode="promise_in_bounds")
            for c in range(0, width, 128)
        ]
        out.append(wide(parts))
    return jnp.stack(out, 0).reshape(labels.shape)


def at_end(q, value):
    end = jnp.where(sublane(q.shape[1:]) == 7, value, q[-1])[None]
    return end if q.shape[0] == 1 else jnp.concatenate([q[:-1], end], 0)


def faces(half_inverse):
    return at_end(1.0 / (half_inverse + following(half_inverse, half_inverse[0])), 0.0)


def factor(e, damping):
    g = jnp.full(e.shape, damping, jnp.float32)
    levels = []
    g_end = jnp.zeros(e.shape[1:], jnp.float32)
    top = True
    while e.shape[0] > 1:
        e_even, e_odd = split(e)
        g_even, g_odd = split(g)
        r = 1.0 / (e_even + e_odd + g_odd)
        if top:
            r = at_end(r, 0.0)
            right = at_end(e_odd * r, 1.0)
        else:
            right = e_odd * r
        left = e_even * r
        top = False
        levels.append((left, right, r))
        e = e_even * right
        moved, wrap = preceding(right * g_odd)
        g = g_even + left * g_odd + moved
        g_end = g_end + wrap
    e, g = e[0], g[0]
    sub = sublane(e.shape)
    for by in (1, 2, 4):
        chosen = sub % (2 * by) == by
        e_left = turn(e, by)
        r = jnp.where(chosen, 1.0 / (e_left + e + g), 0.0)
        left, right = e_left * r, e * r
        levels.append((left, right, r))
        e = e * turn(right, -by)
        wrap = turn(right * g, by)
        g = g + turn(left * g, -by) + jnp.where(sub == 0, 0.0, wrap)
        g_end = g_end + wrap
    return levels, e, g, g_end


def forward(levels, f):
    kept = []
    f_end = jnp.zeros(f.shape[1:], jnp.float32)
    for left, right, r in levels[:-3]:
        f_even, f_odd = split(f)
        kept.append(f_odd)
        moved, wrap = preceding(right * f_odd)
        f = f_even + left * f_odd + moved
        f_end = f_end + wrap
    f = f[0]
    sub = sublane(f.shape)
    for by, (left, right, r) in zip((1, 2, 4), levels[-3:]):
        kept.append(f)
        wrap = turn(right * f, by)
        f = f + turn(left * f, -by) + jnp.where(sub == 0, 0.0, wrap)
        f_end = f_end + wrap
    return kept, f, f_end


def backward(levels, kept, first, last):
    shape = levels[-1][2].shape
    sub = sublane(shape)
    kept = [None] * len(levels) if kept is None else kept
    v = jnp.broadcast_to(first, shape)
    last = jnp.broadcast_to(last, shape)

    def between(level, own, low, high):
        left, right, r = level
        inner = left * low + right * high
        return inner if own is None else own * r + inner

    for by, level, own in zip((4, 2, 1), levels[:-4:-1], kept[:-4:-1]):
        after = jnp.where(sub >= 8 - by, last, turn(v, -by))
        v = jnp.where(sub % (2 * by) == by, between(level, own, turn(v, by), after), v)
    v = v[None]
    for level, own in zip(levels[:-3][::-1], kept[:-3][::-1]):
        v = merge(v, between(level, own, v, following(v, last)))
    return v


def homogeneous(levels):
    row = jnp.zeros_like(levels[-1][2][0:1])
    return backward(levels, None, row + 1.0, row), backward(levels, None, row, row + 1.0)


def central(k):
    return following(k, jnp.zeros_like(k[0])) - preceding(k)[0]


def matrix_rows(e, g, g_end, k, a, b):
    return [e[0:1], g[0:1], g_end[0:1]] + [q for x in (k, a, b) for q in (x[0, 0:1], x[-1, 7:8])]


def put_record(box, me, rows):
    for q, row in enumerate(rows):
        box[q, pl.ds(me, 1), :] = row


def partner(me, mask, n):
    if n & (n - 1):
        return lax.rem(me + mask, n)
    out = me
    bit = 1
    while bit < n:
        if mask & bit:
            out = out + bit * (1 - 2 * lax.rem(lax.div(me, bit), 2))
        bit *= 2
    return out


def send_all(box, me, n, axis, send, recv, begin=0, end=None):
    slot = box.at[:, pl.ds(place(me, n), 1), :]
    for k in range(begin, n - 1 if end is None else end):
        pltpu.make_async_remote_copy(
            src_ref=slot,
            dst_ref=slot,
            send_sem=send,
            recv_sem=recv,
            device_id={axis: k + lax.div(k - me + n, n)},
            device_id_type=MESH,
        ).start()


def wait_all(box, n, sem):
    rest = box.at[:, pl.ds(0, n - 1), :]
    pltpu.make_async_copy(rest, rest, sem).wait()


def get_row(box, n, q):
    if n >= 8:
        return box[q]
    width = box.shape[-1]
    sub = sublane((8, width)) % n
    out = jnp.broadcast_to(box[q, 0:1, :], (8, width))
    for i in range(1, n):
        out = jnp.where(sub == i, jnp.broadcast_to(box[q, i : i + 1, :], (8, width)), out)
    return out


def place(me, n):
    return me if n < 16 else lax.rem(me, 2) * (n // 2) + lax.div(me, 2)


def circle(x, by):
    size = x.shape[0]
    if size < 16:
        return turn(x, by)
    low, high = x[: size // 2], x[size // 2 :]
    if by % 2 == 0:
        return jnp.concatenate([turn(low, by // 2), turn(high, by // 2)], 0)
    if by == 1:
        return jnp.concatenate([turn(high, 1), low], 0)
    return jnp.concatenate([high, turn(low, -1)], 0)


def ring_factor(box, n):
    e, g, g_end, k_head, k_tail, a_head, a_tail, b_head, b_tail = [get_row(box, n, q) for q in range(9)]
    series = k_tail + circle(k_head, -1)
    link = 1.0 / series
    gain = [link, circle(a_head, -1), circle(b_head, -1)]
    loss = [circle(link, 1), circle(a_tail, 1), circle(b_tail, 1)]
    right = 1.0 / (series * (e + g_end) + 1.0)
    r = series * right
    left = e * r
    g = g + left * g_end + circle(right * g_end, 1)
    e = e * right
    levels = []
    by = 1
    while by < n:
        e_left = circle(e, by)
        s = 1.0 / (e_left + e + g)
        lo, hi = e_left * s, e * s
        levels.append((by, lo, hi))
        g = g + circle(lo * g, -by) + circle(hi * g, by)
        e = e * circle(hi, -by)
        by *= 2
    return gain, loss, r, left, right, levels, 1.0 / g


def ring_solve(box, n, ring, order, me, first_out, last_out):
    gain, loss, r, left, right, levels, inv = ring
    size = inv.shape[0]
    for i, which in enumerate(order):
        end = get_row(box, n, 3 + i) + gain[which]
        v = get_row(box, n, i) - loss[which] + left * end + circle(right * end, 1)
        for by, lo, hi in levels:
            v = v + circle(lo * v, -by) + circle(hi * v, by)
        v = v * inv
        first_out[i * size : (i + 1) * size, :] = v
        last_out[i * size : (i + 1) * size, :] = r * end + left * v + right * circle(v, -1)
    return [
        (first_out[pl.ds(i * size + me, 1), :], last_out[pl.ds(i * size + me, 1), :]) for i in range(3)
    ]


def stacked(rows):
    shape = (8, rows[0].shape[1])
    out = jnp.zeros(shape, jnp.float32)
    for i, row in enumerate(rows):
        out = jnp.where(sublane(shape) == i, row, out)
    return out


def total(x):
    x = jnp.sum(x, axis=0) if x.ndim == 3 else x
    for by in (1, 2, 4):
        x = x + turn(x, by)
    return x[0:1]


def kernel(nx, ny, damping, pot_hbm, lab_hbm, pri_hbm, off_hbm, own_out, first_out, last_out, ends_out, pot, lab, pri, off, box_x, mat_y, box_y,
           labt, ft, first_x, last_x, first_y, last_y, send_x, recv_x, send_y, recv_y, load):
    me_x, me_y = lax.axis_index("gx"), lax.axis_index("gy")
    loads, steps, _, cols = pot.shape
    rows = steps * 8
    small = [pltpu.make_async_copy(src, dst, load.at[i]) for i, (src, dst) in enumerate(((pri_hbm, pri), (off_hbm, off)), 1)]
    for copy in small:
        copy.start()
    for s in range(8):
        pltpu.make_async_copy(lab_hbm.at[pl.ds(s * steps, steps), :], lab.at[:, s, :], load.at[0]).start()
    barrier = pltpu.get_barrier_semaphore()
    for mask in range(nx - 1, 0, -1):
        pl.semaphore_signal(barrier, inc=1, device_id={"gx": partner(me_x, mask, nx)}, device_id_type=MESH)
    for mask in range(1, ny):
        pl.semaphore_signal(barrier, inc=1, device_id={"gy": partner(me_y, mask, ny)}, device_id_type=MESH)
    for s in range(8):
        pltpu.make_async_copy(pot_hbm.at[:, pl.ds(s * steps, steps), :], pot.at[:, :, s, :], load.at[3]).start()

    for copy in small:
        copy.wait()
    kx_table, ky_table = 0.5 / spread(pri, 0), 0.5 / spread(pri, 1)
    xy_table, xz_table, yz_table = [0.5 * spread(off, row) for row in range(3)]
    pltpu.make_async_copy(lab, lab, load.at[0]).wait()
    labels = lab[...]
    k = lookup(kx_table, labels)
    e = faces(k)
    pltpu.make_async_copy(pot, pot, load.at[3]).wait()
    levels, e_in, g, g_end = factor(e, damping)
    a, b = lookup(xy_table, labels), lookup(xz_table, labels)
    source = [e - preceding(e)[0], central(a), central(b)]
    solved = [forward(levels, damping * pot[i] + source[i]) for i in range(3)]
    put_record(box_x, place(me_x, nx), matrix_rows(e_in, g, g_end, k, a, b) + [s[1][0:1] for s in solved] + [s[2][0:1] for s in solved])
    pl.semaphore_wait(barrier, nx - 1 + ny - 1)
    send_all(box_x, me_x, nx, "gx", send_x.at[0], recv_x.at[0], 0, 4)

    lanes = labt.shape[0] * 128
    repeat = lanes // rows

    def across(q):
        flat = q.reshape(rows, cols)
        if repeat > 1:
            flat = jnp.concatenate([flat] * repeat, 0)
        return flat.T

    def along(q, slot):
        for t in range(ysteps):
            for c in range(lanes // 128):
                ft[slot, c, pl.ds(t, 8, stride=ysteps), :] = q[t, :, c * 128 : (c + 1) * 128]
        return get_wide(ft.at[slot])

    put_wide(labt, across(labels))
    ysteps = cols // 8
    labels_y = strided_wide(labt, ysteps)
    ky, ay, by = [lookup(table, labels_y) for table in (ky_table, xy_table, yz_table)]
    ey = faces(ky)
    levels_y, ey_in, gy, gy_end = factor(ey, damping)
    put_record(mat_y, me_y, matrix_rows(ey_in, gy, gy_end, ky, ay, by))
    send_all(box_x, me_x, nx, "gx", send_x.at[0], recv_x.at[0], 4)
    send_all(mat_y, me_y, ny, "gy", send_y.at[0], recv_y.at[0])
    source_y = [central(ay), ey - preceding(ey)[0], central(by)]
    base_y = [forward(levels_y, q) for q in source_y]
    zero = jnp.zeros((1, cols), jnp.float32)
    inner = [backward(levels, kept, zero, zero) for kept, _, _ in solved]
    first_part, last_part = homogeneous(levels)
    first_y_part, last_y_part = homogeneous(levels_y)
    first_share, last_share = along(first_y_part, 0), along(last_y_part, 1)
    first_out[...], last_out[...] = first_share, last_share
    first_weight, last_weight = damping * first_share, damping * last_share
    turned = [across(q) for q in inner]
    base_firsts = [base_y[i][1][0:1] + total((first_weight * turned[i]).reshape(ysteps, 8, lanes)) for i in range(3)]
    base_lasts = [base_y[i][2][0:1] + total((last_weight * turned[i]).reshape(ysteps, 8, lanes)) for i in range(3)]
    parts = [across(first_part), across(last_part)]
    response = jnp.concatenate([jnp.concatenate([w * q for w in (first_weight, last_weight)], 1) for q in parts], 0)
    response_hi = response.astype(jnp.bfloat16)
    response_lo = (response - response_hi.astype(jnp.float32)).astype(jnp.bfloat16)

    wait_all(mat_y, ny, recv_y.at[0])
    ring_y = ring_factor(mat_y, ny)
    wait_all(box_x, nx, recv_x.at[0])
    ring_x = ring_factor(box_x, nx)
    ends = ring_solve(box_x.at[pl.ds(9, 6)], nx, ring_x, (0, 1, 2), place(me_x, nx), first_x, last_x)
    vector = jnp.concatenate([stacked([ends[i][0] for i in range(3)]), stacked([ends[i][1] for i in range(3)])], 1)
    coarse = vector.astype(jnp.bfloat16).astype(jnp.float32)
    operand = jnp.concatenate([coarse, vector - coarse], 0).astype(jnp.bfloat16)
    response = jnp.dot(operand, response_hi, preferred_element_type=jnp.float32)
    response = response[:8] + response[8:] + jnp.dot(operand, response_lo, preferred_element_type=jnp.float32)[:8]
    firsts = [base_firsts[i] + response[i : i + 1, :lanes] for i in range(3)]
    lasts = [base_lasts[i] + response[i : i + 1, lanes:] for i in range(3)]
    put_record(box_y, me_y, firsts + lasts)
    send_all(box_y, me_y, ny, "gy", send_y.at[1], recv_y.at[1])

    row = jnp.zeros((1, lanes), jnp.float32)
    for i in range(3):
        put_wide(ft.at[2 + i], turned[i] + across(first_part * ends[i][0] + last_part * ends[i][1]))
        kept = forward(levels_y, damping * strided_wide(ft.at[2 + i], ysteps) + source_y[i])[0]
        own_out[i] = along(backward(levels_y, kept, row, row), 2 + i).T[:rows].reshape(steps, 8, cols)
    wait_all(box_y, ny, recv_y.at[1])
    ends = ring_solve(box_y, ny, ring_y, (1, 0, 2), me_y, first_y, last_y)
    for i in range(3):
        ends_out[2 * i : 2 * i + 1, :] = ends[i][0]
        ends_out[2 * i + 1 : 2 * i + 2, :] = ends[i][1]
    for box, n, sem in ((box_x, nx, send_x.at[0]), (mat_y, ny, send_y.at[0]), (box_y, ny, send_y.at[1])):
        wait_all(box, n, sem)


def store(own, first, last, ends, out, v, sem):
    loads, steps, _, cols = v.shape
    for i in range(loads):
        change = first[...] * ends[2 * i : 2 * i + 1, :] + last[...] * ends[2 * i + 1 : 2 * i + 2, :]
        v[i] = own[i] + change.T[: steps * 8].reshape(steps, 8, cols)
        for s in range(8):
            pltpu.make_async_copy(v.at[i, :, s, :], out.at[i, pl.ds(s * steps, steps), :], sem).start()
    pltpu.make_async_copy(v, v, sem).wait()


def local(potential, labels, principal, off_diagonal):
    nx, ny = lax.axis_size("gx"), lax.axis_size("gy")
    loads, _, rows, cols = potential.shape
    lanes = max(rows, 128)
    steps = rows // 8
    damping = 2.0 / (cols * cols)
    vmem = pl.BlockSpec(memory_space=pltpu.VMEM)
    hbm = pl.BlockSpec(memory_space=pltpu.HBM)
    args = (potential.reshape(loads, rows, cols), labels.reshape(rows, cols), principal, off_diagonal)
    result = pl.pallas_call(
        functools.partial(kernel, nx, ny, damping),
        out_shape=[
            pltpu.VMEM(shape, jnp.float32)
            for shape in ((loads, steps, 8, cols), (cols, lanes), (cols, lanes), (2 * loads, lanes))
        ],
        in_specs=[hbm] * 4,
        out_specs=[vmem] * 4,
        scratch_shapes=[
            pltpu.VMEM((loads, steps, 8, cols), jnp.float32),
            pltpu.VMEM((steps, 8, cols), jnp.int32),
            pltpu.SMEM(principal.shape, jnp.float32),
            pltpu.SMEM(off_diagonal.shape, jnp.float32),
            pltpu.VMEM((15, nx, cols), jnp.float32),
            pltpu.VMEM((9, ny, lanes), jnp.float32),
            pltpu.VMEM((6, ny, lanes), jnp.float32),
            pltpu.VMEM((lanes // 128, cols, 128), jnp.int32),
            pltpu.VMEM((5, lanes // 128, cols, 128), jnp.float32),
            pltpu.VMEM((loads * max(nx, 8), cols), jnp.float32),
            pltpu.VMEM((loads * max(nx, 8), cols), jnp.float32),
            pltpu.VMEM((loads * max(ny, 8), lanes), jnp.float32),
            pltpu.VMEM((loads * max(ny, 8), lanes), jnp.float32),
            pltpu.SemaphoreType.DMA((1,)),
            pltpu.SemaphoreType.DMA((1,)),
            pltpu.SemaphoreType.DMA((2,)),
            pltpu.SemaphoreType.DMA((2,)),
            pltpu.SemaphoreType.DMA((4,)),
        ],
        compiler_params=pltpu.CompilerParams(
            collective_id=0, has_side_effects=True, vmem_limit_bytes=32 * 1024 * 1024
        ),
    )(*[pltpu.with_memory_space_constraint(x, pltpu.HBM) for x in args])
    result = pl.pallas_call(
        store,
        out_shape=pltpu.HBM((loads, rows, cols), jnp.float32),
        in_specs=[vmem] * 4,
        out_specs=hbm,
        scratch_shapes=[pltpu.VMEM((loads, steps, 8, cols), jnp.float32), pltpu.SemaphoreType.DMA],
        compiler_params=pltpu.CompilerParams(vmem_limit_bytes=8 * 1024 * 1024),
    )(*[pltpu.with_memory_space_constraint(x, pltpu.VMEM) for x in result])
    return result.reshape(potential.shape)


def solution(mesh):
    in_specs = (P(None, None, "gx", "gy"), P(None, "gx", "gy"), P(), P())
    out_specs = P(None, None, "gx", "gy")
    return jax.shard_map(local, mesh=mesh, in_specs=in_specs, out_specs=out_specs, check_vma=False)
```
